128 devices in a mesh: row: 16 (over y, x), col: 4 (over z), depth: 2 (over core).
Axes of the slice: x: 4, y: 4, z: 4, core: 2. Of those that a mesh axis runs over, the one named last changes fastest.
Arguments:
- upper: float32 [8192, 8192], P('row', 'col'), may hold values from -0.25 to 0.25
- pattern: int32 [64, 64], replicated, may hold values from 0 to 1, as said below
Outputs:
- purified: float32 [8192, 8192], P('row', 'col')
The draws below stay inside these ranges and needn't reach their ends.
Inputs may be any that keep to these rules, and one draw needn't show every extreme that they name: `pattern`: block pairs near the diagonal are present; a few far pairs are present too.
All inputs are finite; a program needn't handle non-finite values.
Results may differ from the reference program's by a relative error of at most 0.00007.
Values sent between devices are 32-bit elements; how exact they have to be, the bound alone decides.
No kernel may reach another device: no remote copies, remote signals or barrier semaphores. Data moves between devices by JAX's collectives and lax.ppermute only.
A program may use at most 128 MiB of HBM per device.

```python
import jax
import jax.numpy as jnp
from jax import lax

BS = 128
NB = 64


def draw_pattern(key, part):
    near_key = jax.random.fold_in(key, 11)
    far_key = jax.random.fold_in(key, 23)
    block_ids = jnp.arange(NB, dtype=jnp.int32)
    radius = jax.random.randint(near_key, (NB,), 1, 4, dtype=jnp.int32)
    distance = jnp.abs(block_ids[:, None] - block_ids[None, :])
    near = distance <= radius[:, None]
    far = jax.random.randint(far_key, (NB, NB), 0, 16, dtype=jnp.int32) == 0
    return jnp.where(near | far, 1, 0).astype(jnp.int32)


def level_of(rng, shape, cuts, smallest, high):
    loudness, own = 1.0, jax.random.fold_in(rng, 6)
    for dim, blocks in cuts:
        draws = jnp.exp(jax.random.uniform(jax.random.fold_in(own, dim), (blocks,), jnp.float32, smallest / len(cuts), high / len(cuts)))
        loudness = loudness * jnp.repeat(draws, shape[dim] // blocks).reshape([-1 if axis == dim else 1 for axis in range(len(shape))])
    return loudness


def noise(stream_key, shape, width, reach, shards=(), held_as=jnp.bfloat16):
    array = jax.random.normal(stream_key, shape, jnp.float32) * width
    if len(shards) > 0:
        array = level_of(stream_key, shape, shards, -0.22, 0.18) * array
    return jnp.clip(array, min=-reach, max=reach).astype(held_as)


def setup_inputs(seed: int = 0) -> dict:
    key_list = jax.random.split(jax.random.key(seed), 3)
    return {
        "upper": noise(key_list[0], (NB * BS, NB * BS), (NB * BS // 16) ** -0.5, 0.25, ((0, 16), (1, 4)), jnp.float32),
        "pattern": draw_pattern(jax.random.fold_in(key_list[2], 71), 0),
    }


def reference(upper, pattern):
    block_ids = jnp.arange(NB, dtype=jnp.int32)
    above = block_ids[:, None] < block_ids[None, :]
    below = block_ids[:, None] > block_ids[None, :]
    keep = jnp.where(above, pattern, jnp.where(below, pattern.T, 1)).astype(jnp.int32)
    cell_block = jnp.arange(NB * BS, dtype=jnp.int32) // BS
    cell_above = cell_block[:, None] < cell_block[None, :]
    cell_below = cell_block[:, None] > cell_block[None, :]
    mirrored = upper.T
    blended = jnp.where(cell_above, upper, jnp.where(cell_below, mirrored, 0.5 * (upper + mirrored)))
    cell_keep = keep[cell_block[:, None], cell_block[None, :]].astype(jnp.float32)
    density = blended * cell_keep
    square = jnp.dot(density, density, precision=lax.Precision.HIGHEST, preferred_element_type=jnp.float32)
    cube = jnp.dot(square, density, precision=lax.Precision.HIGHEST, preferred_element_type=jnp.float32)
    return 3.0 * square - 2.0 * cube
```

```python
import jax
import jax.numpy as jnp
from jax import lax
from jax.experimental import pallas as pl
from jax.experimental.pallas import tpu as pltpu
from jax.sharding import PartitionSpec as P

BS = 128
NB = 64
ROWS = 4
COLS = 16
NROW = 16
NCOL = 4
STRIPS = 16
PER = 44
CAP = 8 * PER
SRC = 4
HALF = 2
MR = HALF * BS
VMEM = 60 * 1024 * 1024
ALL = ("row", "col", "depth")


def prefix(ones):
    ids = jnp.arange(NB, dtype=jnp.int32)
    before = (ids[:, None] < ids[None, :]).astype(jnp.float32)
    return jnp.dot(ones.astype(jnp.float32), before, preferred_element_type=jnp.float32).astype(jnp.int32)


def layout(pattern):
    ids = jnp.arange(NB, dtype=jnp.int32)
    stored = jnp.where(ids[:, None] < ids[None, :], pattern, 0) + (ids[:, None] == ids[None, :])
    stored = (stored != 0).astype(jnp.int32)
    local = stored.reshape(NROW, ROWS, NCOL, COLS).transpose(0, 2, 1, 3).reshape(NB, NB)
    rank = prefix(local)
    count = jnp.sum(local, axis=1)
    first = prefix(count[None, :])[0]
    last = first + count
    slot = (first[:, None] + rank).reshape(NROW, NCOL, ROWS, COLS).transpose(0, 2, 1, 3).reshape(NB, NB)
    fits = jnp.all(((last - 1) >> 3) - (first >> 3) < SRC) & (last[NB - 1] <= CAP)
    return stored, slot, local, rank, first, last, fits


def pack_kernel(index_ref, upper_ref, out_ref):
    shift = index_ref[16]

    def one(e, _):
        index = index_ref[e]

        @pl.when(index >= 0)
        def _():
            a = index >> 4
            b = index & 15
            x = upper_ref[pl.ds(pl.multiple_of(a * BS, BS), BS), pl.ds(pl.multiple_of(b * BS, BS), BS)]

            @pl.when(a + shift != b)
            def _():
                out_ref[:, e >> 2, e & 3] = x.reshape(STRIPS, 8, BS)

            @pl.when(a + shift == b)
            def _():
                out_ref[:, e >> 2, e & 3] = (0.5 * (x + x.T)).reshape(STRIPS, 8, BS)

        return 0

    lax.fori_loop(0, 16, one, 0)


def select_kernel(index_ref, got_ref, out_ref):
    for u in range(PER):
        out_ref[u] = got_ref[index_ref[u]]


def split(x):
    high = x.astype(jnp.bfloat16)
    return high, (x - high.astype(jnp.float32)).astype(jnp.bfloat16)


def main_kernel(sd_ref, st_ref, sn_ref, pd_ref, pt_ref, pn_ref, row_ref, rn_ref, where_ref, blocks_ref, out_ref,
                a_ref, s_ref, acc_ref):
    first_col = where_ref[0]
    a_ref[...] = jnp.zeros_like(a_ref)
    s_ref[NB] = jnp.zeros((2 * MR, BS), jnp.bfloat16)

    def block(slot):
        return blocks_ref[:, slot & 7, slot >> 3].reshape(BS, BS)

    for h in range(HALF):
        def fill(p, _, h=h):
            code = row_ref[h, p]
            m = code & 127
            x = block((code >> 7) & 511)

            def put(x):
                high, low = split(x)
                a_ref[m, h * BS:(h + 1) * BS] = high
                a_ref[m, MR + h * BS:MR + (h + 1) * BS] = low

            @pl.when(code < 65536)
            def _():
                put(x)

            @pl.when(code >= 65536)
            def _():
                put(x.T)

            return 0

        lax.fori_loop(0, rn_ref[h], fill, 0)

    def product(left_ref, d_ref, t_ref, k, p):
        def operands(ref):
            c0, c1 = ref[k, p], ref[k, p + 1]
            left = jnp.concatenate([left_ref[c0 & 127], left_ref[c1 & 127]], axis=1)
            return left, block(c0 >> 7), block(c1 >> 7)

        left, x0, x1 = operands(d_ref)
        h0, l0 = split(x0)
        h1, l1 = split(x1)
        right = jnp.concatenate([jnp.concatenate([h0, l0], axis=1), jnp.concatenate([h1, l1], axis=1)], axis=0)
        z = jnp.dot(left, right, preferred_element_type=jnp.float32)
        left, x0, x1 = operands(t_ref)
        h0, l0 = split(x0)
        h1, l1 = split(x1)
        right = jnp.concatenate([jnp.concatenate([h0, h1], axis=1), jnp.concatenate([l0, l1], axis=1)], axis=0)
        z += lax.dot_general(left, right, (((1,), (1,)), ((), ())), preferred_element_type=jnp.float32)
        z = z[:MR] + z[MR:]
        return z[:, :BS] + z[:, BS:]

    def square(k, _):
        acc_ref[...] = product(a_ref, sd_ref, st_ref, k, 0)

        def step(i, _):
            acc_ref[...] += product(a_ref, sd_ref, st_ref, k, 2 * i)
            return 0

        lax.fori_loop(1, sn_ref[k], step, 0)
        x = acc_ref[...]
        high, low = split(x)
        s_ref[k, :MR] = high
        s_ref[k, MR:] = low
        j = k - first_col

        @pl.when((j >= 0) & (j < COLS))
        def _():
            out_ref[:, pl.ds(pl.multiple_of(j * BS, BS), BS)] = 3.0 * x

        return 0

    lax.fori_loop(0, NB, square, 0)

    def cube(j, _):
        acc_ref[...] = product(s_ref, pd_ref, pt_ref, j, 0)

        def step(i, _):
            acc_ref[...] += product(s_ref, pd_ref, pt_ref, j, 2 * i)
            return 0

        lax.fori_loop(1, pn_ref[j], step, 0)
        out_ref[:, pl.ds(pl.multiple_of(j * BS, BS), BS)] += -2.0 * acc_ref[...]
        return 0

    lax.fori_loop(0, COLS, cube, 0)


def compact(chosen, codes, pad):
    ids = jnp.arange(NB, dtype=jnp.int32)
    at = jnp.where(chosen, prefix(chosen), -1)
    hit = at[:, :, None] == ids[None, None, :]
    return pad + jnp.sum(jnp.where(hit, (codes - pad)[:, :, None], 0), axis=1)


def pairs(direct, mirrored):
    most = jnp.maximum(jnp.sum(direct.astype(jnp.int32), axis=1), jnp.sum(mirrored.astype(jnp.int32), axis=1))
    return (most + 1) >> 1


SMEM = pl.BlockSpec(memory_space=pltpu.SMEM)
INVMEM = pl.BlockSpec(memory_space=pltpu.VMEM)


def sparse(upper, pattern):
    ids = jnp.arange(NB, dtype=jnp.int32)
    stored, slot, local, rank, first, last, _ = layout(pattern)
    row, col, depth = lax.axis_index("row"), lax.axis_index("col"), lax.axis_index("depth")
    chip = row * NCOL + col
    mine = lax.dynamic_index_in_dim(local, chip, 0, False)
    my_rank = lax.dynamic_index_in_dim(rank, chip, 0, False)
    my_first = lax.dynamic_index_in_dim(first, chip, 0, False)
    entry = jnp.arange(16, dtype=jnp.int32)
    wanted = 8 * ((my_first >> 3) + (entry & 3)) + 2 * (entry >> 2) + depth - my_first
    hit = (my_rank[None, :] == wanted[:, None]) & (mine[None, :] != 0)
    index = jnp.sum(jnp.where(hit, ids[None, :] + 1, 0), axis=1) - 1
    index = jnp.concatenate([index, (row * ROWS - col * COLS)[None]]).astype(jnp.int32)
    packed = pl.pallas_call(
        pack_kernel,
        out_shape=jax.ShapeDtypeStruct((STRIPS, NCOL, SRC, 8, BS), jnp.float32),
        in_specs=[SMEM, INVMEM],
        out_specs=INVMEM,
        compiler_params=pltpu.CompilerParams(vmem_limit_bytes=16 * 1024 * 1024),
    )(index, upper)
    got = lax.all_to_all(packed.reshape(NB, SRC * 8, BS), ("row", "col"), 0, 0, tiled=True)
    u = jnp.arange(PER, dtype=jnp.int32)
    g = 8 * u + 2 * col + depth
    source = jnp.minimum(jnp.sum((last[None, :] <= g[:, None]).astype(jnp.int32), axis=1), NB - 1)
    source_first = jnp.sum(jnp.where(source[:, None] == ids[None, :], first[None, :], 0), axis=1)
    pick = source * SRC + jnp.clip(u - (source_first >> 3), 0, SRC - 1)
    share = pl.pallas_call(
        select_kernel,
        out_shape=jax.ShapeDtypeStruct((PER, 8, BS), jnp.float32),
        in_specs=[SMEM, INVMEM],
        out_specs=INVMEM,
        compiler_params=pltpu.CompilerParams(vmem_limit_bytes=16 * 1024 * 1024),
    )(pick, got.reshape(NB * SRC, 8, BS))
    blocks = lax.all_gather(share, ALL, axis=0).reshape(STRIPS, 8, PER, 8, BS)

    below = ids[:, None] > ids[None, :]
    both = jnp.where(below, stored.T, stored) != 0
    slots = jnp.where(below, slot.T, slot)
    codes = ids[None, :] + BS * slots
    my_row = row * ROWS + depth * HALF
    near = jnp.any(lax.dynamic_slice_in_dim(both, my_row, HALF, 0), axis=0)
    direct = both & (ids[None, :] <= ids[:, None])
    mirrored = both & (ids[None, :] > ids[:, None])
    sd, st = direct & near[None, :], mirrored & near[None, :]
    col_direct = lax.dynamic_slice_in_dim(direct, col * COLS, COLS, 0)
    col_mirrored = lax.dynamic_slice_in_dim(mirrored, col * COLS, COLS, 0)
    col_codes = lax.dynamic_slice_in_dim(codes, col * COLS, COLS, 0)
    row_both = lax.dynamic_slice_in_dim(both, my_row, HALF, 0)
    row_codes = lax.dynamic_slice_in_dim(codes + 65536 * below, my_row, HALF, 0)
    half = pl.pallas_call(
        main_kernel,
        out_shape=jax.ShapeDtypeStruct((MR, COLS * BS), jnp.float32),
        in_specs=[SMEM] * 9 + [INVMEM],
        out_specs=INVMEM,
        scratch_shapes=[
            pltpu.VMEM((NB + 1, 2 * MR, BS), jnp.bfloat16),
            pltpu.VMEM((NB + 1, 2 * MR, BS), jnp.bfloat16),
            pltpu.VMEM((MR, BS), jnp.float32),
        ],
        compiler_params=pltpu.CompilerParams(vmem_limit_bytes=VMEM),
    )(
        compact(sd, codes, NB), compact(st, codes, NB), pairs(sd, st),
        compact(col_direct, col_codes, NB), compact(col_mirrored, col_codes, NB), pairs(col_direct, col_mirrored),
        compact(row_both, row_codes, NB), jnp.sum(row_both.astype(jnp.int32), axis=1),
        (col * COLS)[None].astype(jnp.int32), blocks,
    )
    return lax.all_gather(half, "depth", axis=0, tiled=True)


def dense(upper, pattern):
    rows_tile, cols_tile = upper.shape
    nrow = lax.axis_size("row")
    ncol = lax.axis_size("col")
    ndep = lax.axis_size("depth")
    row_blocks = rows_tile // BS
    col_blocks = cols_tile // BS
    spread = upper.reshape(row_blocks, ncol, BS // ncol, col_blocks, nrow, BS // nrow)
    spread = spread.transpose(4, 1, 0, 2, 3, 5).reshape(
        nrow * ncol, row_blocks, BS // ncol, col_blocks, BS // nrow
    )
    spread = lax.all_to_all(spread, ("row", "col"), split_axis=0, concat_axis=0, tiled=True)
    spread = spread.reshape(nrow, ncol, row_blocks, BS // ncol, col_blocks, BS // nrow)
    spread = spread.transpose(0, 2, 3, 1, 4, 5).reshape(
        ncol, col_blocks, BS // ncol, nrow, row_blocks, BS // nrow
    )
    spread = spread.transpose(3, 0, 4, 5, 1, 2).reshape(
        nrow * ncol, row_blocks, BS // nrow, col_blocks, BS // ncol
    )
    spread = lax.all_to_all(spread, ("row", "col"), split_axis=0, concat_axis=0, tiled=True)
    spread = spread.reshape(nrow, ncol, row_blocks, BS // nrow, col_blocks, BS // ncol)
    mirror = spread.transpose(2, 0, 3, 4, 1, 5).reshape(row_blocks, BS, col_blocks, BS)
    row_index = lax.axis_index("row")
    col_index = lax.axis_index("col")
    row_first = row_index * row_blocks
    col_first = col_index * col_blocks
    global_rows = row_first + jnp.arange(row_blocks, dtype=jnp.int32)
    global_cols = col_first + jnp.arange(col_blocks, dtype=jnp.int32)
    above = global_rows[:, None] < global_cols[None, :]
    below = global_rows[:, None] > global_cols[None, :]
    upper_pat = lax.dynamic_slice(pattern, (row_first, col_first), (row_blocks, col_blocks))
    lower_pat = lax.dynamic_slice(pattern, (col_first, row_first), (col_blocks, row_blocks)).T
    keep = jnp.where(above, upper_pat, jnp.where(below, lower_pat, 1)).astype(jnp.float32)
    own = upper.reshape(row_blocks, BS, col_blocks, BS)
    blended = jnp.where(
        above[:, None, :, None],
        own,
        jnp.where(below[:, None, :, None], mirror, 0.5 * (own + mirror)),
    )
    density = (blended * keep[:, None, :, None]).reshape(rows_tile, cols_tile)
    layer = lax.axis_index("depth")

    def layer_columns(tile):
        split = tile.reshape(rows_tile, col_blocks // ndep, ndep, BS)
        return lax.dynamic_slice_in_dim(split, layer, 1, 2).reshape(
            rows_tile, col_blocks // ndep * BS
        )

    split_rows = density.reshape(row_blocks // ndep, ndep, BS, cols_tile)
    layer_rows = lax.dynamic_slice_in_dim(split_rows, layer, 1, 1).reshape(
        row_blocks // ndep * BS, cols_tile
    )
    panel = lax.all_gather(layer_rows, "row", axis=0, tiled=True)

    def accumulate(piece):
        return jnp.dot(
            piece, panel, precision=lax.Precision.HIGHEST, preferred_element_type=jnp.float32
        )

    square_part = accumulate(lax.all_gather(layer_columns(density), "col", axis=1, tiled=True))
    square = lax.psum(square_part, "depth")
    cube_part = accumulate(lax.all_gather(layer_columns(square), "col", axis=1, tiled=True))
    cube = lax.psum(cube_part, "depth")
    return 3.0 * square - 2.0 * cube


def local(upper, pattern):
    return lax.cond(layout(pattern)[-1], sparse, dense, upper, pattern)


def solution(mesh):
    placed = (P("row", "col"), P())
    return jax.shard_map(
        local, mesh=mesh, in_specs=placed, out_specs=P("row", "col"), check_vma=False
    )
```

```python
import jax
import jax.numpy as jnp
from jax import lax
from jax.experimental import pallas as pl
from jax.experimental.pallas import tpu as pltpu
from jax.sharding import PartitionSpec as P

BS = 128
NB = 64
ROWS = 4
COLS = 16
NROW = 16
NCOL = 4
STRIPS = 16
PER = 44
CAP = 8 * PER
SRC = 4
HALF = 2
MR = HALF * BS
UNROLL = 8
VMEM = 62 * 1024 * 1024
ALL = ("row", "col", "depth")


def prefix(ones):
    ids = jnp.arange(NB, dtype=jnp.int32)
    before = (ids[:, None] < ids[None, :]).astype(jnp.float32)
    return jnp.dot(ones.astype(jnp.float32), before, preferred_element_type=jnp.float32).astype(jnp.int32)


def layout(pattern):
    ids = jnp.arange(NB, dtype=jnp.int32)
    stored = jnp.where(ids[:, None] < ids[None, :], pattern, 0) + (ids[:, None] == ids[None, :])
    stored = (stored != 0).astype(jnp.int32)
    local = stored.reshape(NROW, ROWS, NCOL, COLS).transpose(0, 2, 1, 3).reshape(NB, NB)
    rank = prefix(local)
    count = jnp.sum(local, axis=1)
    first = prefix(count[None, :])[0]
    last = first + count
    slot = (first[:, None] + rank).reshape(NROW, NCOL, ROWS, COLS).transpose(0, 2, 1, 3).reshape(NB, NB)
    fits = jnp.all(((last - 1) >> 3) - (first >> 3) < SRC) & (last[NB - 1] <= CAP)
    return stored, slot, local, rank, first, last, fits


def pack_kernel(index_ref, upper_ref, out_ref):
    shift = index_ref[16]

    def one(e, _):
        index = index_ref[e]

        @pl.when(index >= 0)
        def _():
            a = index >> 4
            b = index & 15
            x = upper_ref[pl.ds(pl.multiple_of(a * BS, BS), BS), pl.ds(pl.multiple_of(b * BS, BS), BS)]

            @pl.when(a + shift != b)
            def _():
                out_ref[:, e >> 2, e & 3] = x.reshape(STRIPS, 8, BS)

            @pl.when(a + shift == b)
            def _():
                out_ref[:, e >> 2, e & 3] = (0.5 * (x + x.T)).reshape(STRIPS, 8, BS)

        return 0

    lax.fori_loop(0, 16, one, 0)


def select_kernel(index_ref, got_ref, out_ref):
    for u in range(PER):
        out_ref[u] = got_ref[index_ref[u]]


def split(x):
    high = x.astype(jnp.bfloat16)
    return high, (x - high.astype(jnp.float32)).astype(jnp.bfloat16)


def main_kernel(sd_ref, sdn_ref, st_ref, stn_ref, pd_ref, pdn_ref, pt_ref, ptn_ref, row_ref, rn_ref, where_ref,
                blocks_hbm, out_ref, blocks_ref, a_ref, s_ref, sum_ref, cube_ref, item_ref, sem):
    first_col = where_ref[0]
    loads = [
        pltpu.make_async_copy(blocks_hbm.at[pl.ds(2 * i, 2)], blocks_ref.at[pl.ds(2 * i, 2)], sem.at[i])
        for i in range(STRIPS // 2)
    ]
    for load in loads:
        load.start()
    a_ref[...] = jnp.zeros_like(a_ref)
    sum_ref[...] = jnp.zeros_like(sum_ref)
    cube_ref[...] = jnp.zeros_like(cube_ref)
    s_ref[NB] = jnp.zeros((2 * MR, BS), jnp.bfloat16)

    def list_items(count_ref, columns, at):
        def column(k, n):
            def one(i, n):
                item_ref[at, n] = k * NB + 2 * i
                return n + 1

            return lax.fori_loop(0, (count_ref[k] + 1) >> 1, one, n)

        n = lax.fori_loop(0, columns, column, 0)
        for i in range(UNROLL - 1):
            item_ref[at, n + i] = columns * NB
        return (n + UNROLL - 1) // UNROLL

    def block(slot):
        return blocks_ref[:, slot & 7, slot >> 3].reshape(BS, BS)

    rounds = [list_items(sdn_ref, NB, 0), list_items(stn_ref, NB, 1), list_items(pdn_ref, COLS, 2), list_items(ptn_ref, COLS, 3)]
    for load in loads:
        load.wait()

    for h in range(HALF):
        def fill(p, _, h=h):
            code = row_ref[h, p]
            m = code & 127
            x = block((code >> 7) & 511)

            def put(x):
                high, low = split(x)
                a_ref[m, h * BS:(h + 1) * BS] = high
                a_ref[m, MR + h * BS:MR + (h + 1) * BS] = low

            @pl.when(code < 65536)
            def _():
                put(x)

            @pl.when(code >= 65536)
            def _():
                put(x.T)

            return 0

        lax.fori_loop(0, rn_ref[h], fill, 0)

    def product(left_ref, list_ref, mirrored, k, p):
        c0, c1 = list_ref[k, p], list_ref[k, p + 1]
        left = jnp.concatenate([left_ref[c0 & 127], left_ref[c1 & 127]], axis=1)
        h0, l0 = split(block(c0 >> 7))
        h1, l1 = split(block(c1 >> 7))
        if mirrored:
            right = jnp.concatenate([jnp.concatenate([h0, h1], axis=1), jnp.concatenate([l0, l1], axis=1)], axis=0)
            z = lax.dot_general(left, right, (((1,), (1,)), ((), ())), preferred_element_type=jnp.float32)
        else:
            right = jnp.concatenate([jnp.concatenate([h0, l0], axis=1), jnp.concatenate([h1, l1], axis=1)], axis=0)
            z = jnp.dot(left, right, preferred_element_type=jnp.float32)
        z = z[:MR] + z[MR:]
        return z[:, :BS] + z[:, BS:]

    def work(left_ref, list_ref, mirrored, into_ref, at):
        def several(i, _):
            items = [item_ref[at, UNROLL * i + e] for e in range(UNROLL)]
            done = [product(left_ref, list_ref, mirrored, item >> 6, item & 63) for item in items]
            for item, z in zip(items, done):
                into_ref[item >> 6] += z
            return 0

        lax.fori_loop(0, rounds[at], several, 0)

    work(a_ref, sd_ref, False, sum_ref, 0)
    work(a_ref, st_ref, True, sum_ref, 1)

    def halves(k, _):
        high, low = split(sum_ref[k])
        s_ref[k, :MR] = high
        s_ref[k, MR:] = low
        return 0

    lax.fori_loop(0, NB, halves, 0, unroll=2)
    work(s_ref, pd_ref, False, cube_ref, 2)
    work(s_ref, pt_ref, True, cube_ref, 3)
    for j in range(COLS):
        out_ref[:, j * BS:(j + 1) * BS] = 3.0 * sum_ref[first_col + j] - 2.0 * cube_ref[j]


def compact(chosen, codes, pad):
    ids = jnp.arange(NB, dtype=jnp.int32)
    at = jnp.where(chosen, prefix(chosen), -1)
    hit = at[:, :, None] == ids[None, None, :]
    table = pad + jnp.sum(jnp.where(hit, (codes - pad)[:, :, None], 0), axis=1)
    return jnp.pad(table, ((0, 1), (0, 0)), constant_values=pad)


def count(chosen):
    return jnp.sum(chosen.astype(jnp.int32), axis=1)


SMEM = pl.BlockSpec(memory_space=pltpu.SMEM)
INVMEM = pl.BlockSpec(memory_space=pltpu.VMEM)


def sparse(upper, pattern, stored, slot, local, rank, first, last):
    ids = jnp.arange(NB, dtype=jnp.int32)
    row, col, depth = lax.axis_index("row"), lax.axis_index("col"), lax.axis_index("depth")
    chip = row * NCOL + col
    mine = lax.dynamic_index_in_dim(local, chip, 0, False)
    my_rank = lax.dynamic_index_in_dim(rank, chip, 0, False)
    my_first = lax.dynamic_index_in_dim(first, chip, 0, False)
    entry = jnp.arange(16, dtype=jnp.int32)
    wanted = 8 * ((my_first >> 3) + (entry & 3)) + 2 * (entry >> 2) + depth - my_first
    hit = (my_rank[None, :] == wanted[:, None]) & (mine[None, :] != 0)
    index = jnp.sum(jnp.where(hit, ids[None, :] + 1, 0), axis=1) - 1
    index = jnp.concatenate([index, (row * ROWS - col * COLS)[None]]).astype(jnp.int32)
    packed = pl.pallas_call(
        pack_kernel,
        out_shape=jax.ShapeDtypeStruct((STRIPS, NCOL, SRC, 8, BS), jnp.float32),
        in_specs=[SMEM, INVMEM],
        out_specs=INVMEM,
        compiler_params=pltpu.CompilerParams(vmem_limit_bytes=16 * 1024 * 1024),
    )(index, upper)
    got = lax.all_to_all(packed.reshape(NB, SRC * 8, BS), ("row", "col"), 0, 0, tiled=True)
    u = jnp.arange(PER, dtype=jnp.int32)
    g = 8 * u + 2 * col + depth
    source = jnp.minimum(jnp.sum((last[None, :] <= g[:, None]).astype(jnp.int32), axis=1), NB - 1)
    source_first = jnp.sum(jnp.where(source[:, None] == ids[None, :], first[None, :], 0), axis=1)
    pick = source * SRC + jnp.clip(u - (source_first >> 3), 0, SRC - 1)
    share = pl.pallas_call(
        select_kernel,
        out_shape=jax.ShapeDtypeStruct((PER, 8, BS), jnp.float32),
        in_specs=[SMEM, INVMEM],
        out_specs=INVMEM,
        compiler_params=pltpu.CompilerParams(vmem_limit_bytes=16 * 1024 * 1024),
    )(pick, got.reshape(NB * SRC, 8, BS))
    blocks = lax.all_gather(share, ALL, axis=0).reshape(STRIPS, 8, PER, 8, BS)

    half = multiply(blocks, stored, slot)
    return half, lax.ppermute(half, "depth", [(0, 1), (1, 0)])


def multiply(blocks, stored, slot):
    ids = jnp.arange(NB, dtype=jnp.int32)
    row, col, depth = lax.axis_index("row"), lax.axis_index("col"), lax.axis_index("depth")
    below = ids[:, None] > ids[None, :]
    both = jnp.where(below, stored.T, stored) != 0
    slots = jnp.where(below, slot.T, slot)
    codes = ids[None, :] + BS * slots
    my_row = row * ROWS + depth * HALF
    near = jnp.any(lax.dynamic_slice_in_dim(both, my_row, HALF, 0), axis=0)
    direct = both & (ids[None, :] <= ids[:, None])
    mirrored = both & (ids[None, :] > ids[:, None])
    sd, st = direct & near[None, :], mirrored & near[None, :]
    col_direct = lax.dynamic_slice_in_dim(direct, col * COLS, COLS, 0)
    col_mirrored = lax.dynamic_slice_in_dim(mirrored, col * COLS, COLS, 0)
    col_codes = lax.dynamic_slice_in_dim(codes, col * COLS, COLS, 0)
    row_both = lax.dynamic_slice_in_dim(both, my_row, HALF, 0)
    row_codes = lax.dynamic_slice_in_dim(codes + 65536 * below, my_row, HALF, 0)
    return pl.pallas_call(
        main_kernel,
        out_shape=jax.ShapeDtypeStruct((MR, COLS * BS), jnp.float32),
        in_specs=[SMEM] * 11 + [pl.BlockSpec(memory_space=pl.ANY)],
        out_specs=INVMEM,
        scratch_shapes=[
            pltpu.VMEM((STRIPS, 8, PER, 8, BS), jnp.float32),
            pltpu.VMEM((NB + 1, 2 * MR, BS), jnp.bfloat16),
            pltpu.VMEM((NB + 1, 2 * MR, BS), jnp.bfloat16),
            pltpu.VMEM((NB + 1, MR, BS), jnp.float32),
            pltpu.VMEM((COLS + 1, MR, BS), jnp.float32),
            pltpu.SMEM((4, NB * NB // 2 + NB + UNROLL), jnp.int32),
            pltpu.SemaphoreType.DMA((STRIPS // 2,)),
        ],
        compiler_params=pltpu.CompilerParams(vmem_limit_bytes=VMEM),
    )(
        compact(sd, codes, NB), count(sd), compact(st, codes, NB), count(st),
        compact(col_direct, col_codes, NB), count(col_direct), compact(col_mirrored, col_codes, NB), count(col_mirrored),
        compact(row_both, row_codes, NB), count(row_both), (col * COLS)[None].astype(jnp.int32), blocks,
    )


def dense(upper, pattern):
    rows_tile, cols_tile = upper.shape
    nrow = lax.axis_size("row")
    ncol = lax.axis_size("col")
    ndep = lax.axis_size("depth")
    row_blocks = rows_tile // BS
    col_blocks = cols_tile // BS
    spread = upper.reshape(row_blocks, ncol, BS // ncol, col_blocks, nrow, BS // nrow)
    spread = spread.transpose(4, 1, 0, 2, 3, 5).reshape(
        nrow * ncol, row_blocks, BS // ncol, col_blocks, BS // nrow
    )
    spread = lax.all_to_all(spread, ("row", "col"), split_axis=0, concat_axis=0, tiled=True)
    spread = spread.reshape(nrow, ncol, row_blocks, BS // ncol, col_blocks, BS // nrow)
    spread = spread.transpose(0, 2, 3, 1, 4, 5).reshape(
        ncol, col_blocks, BS // ncol, nrow, row_blocks, BS // nrow
    )
    spread = spread.transpose(3, 0, 4, 5, 1, 2).reshape(
        nrow * ncol, row_blocks, BS // nrow, col_blocks, BS // ncol
    )
    spread = lax.all_to_all(spread, ("row", "col"), split_axis=0, concat_axis=0, tiled=True)
    spread = spread.reshape(nrow, ncol, row_blocks, BS // nrow, col_blocks, BS // ncol)
    mirror = spread.transpose(2, 0, 3, 4, 1, 5).reshape(row_blocks, BS, col_blocks, BS)
    row_index = lax.axis_index("row")
    col_index = lax.axis_index("col")
    row_first = row_index * row_blocks
    col_first = col_index * col_blocks
    global_rows = row_first + jnp.arange(row_blocks, dtype=jnp.int32)
    global_cols = col_first + jnp.arange(col_blocks, dtype=jnp.int32)
    above = global_rows[:, None] < global_cols[None, :]
    below = global_rows[:, None] > global_cols[None, :]
    upper_pat = lax.dynamic_slice(pattern, (row_first, col_first), (row_blocks, col_blocks))
    lower_pat = lax.dynamic_slice(pattern, (col_first, row_first), (col_blocks, row_blocks)).T
    keep = jnp.where(above, upper_pat, jnp.where(below, lower_pat, 1)).astype(jnp.float32)
    own = upper.reshape(row_blocks, BS, col_blocks, BS)
    blended = jnp.where(
        above[:, None, :, None],
        own,
        jnp.where(below[:, None, :, None], mirror, 0.5 * (own + mirror)),
    )
    density = (blended * keep[:, None, :, None]).reshape(rows_tile, cols_tile)
    layer = lax.axis_index("depth")

    def layer_columns(tile):
        split = tile.reshape(rows_tile, col_blocks // ndep, ndep, BS)
        return lax.dynamic_slice_in_dim(split, layer, 1, 2).reshape(
            rows_tile, col_blocks // ndep * BS
        )

    split_rows = density.reshape(row_blocks // ndep, ndep, BS, cols_tile)
    layer_rows = lax.dynamic_slice_in_dim(split_rows, layer, 1, 1).reshape(
        row_blocks // ndep * BS, cols_tile
    )
    panel = lax.all_gather(layer_rows, "row", axis=0, tiled=True)

    def accumulate(piece):
        return jnp.dot(
            piece, panel, precision=lax.Precision.HIGHEST, preferred_element_type=jnp.float32
        )

    square_part = accumulate(lax.all_gather(layer_columns(density), "col", axis=1, tiled=True))
    square = lax.psum(square_part, "depth")
    cube_part = accumulate(lax.all_gather(layer_columns(square), "col", axis=1, tiled=True))
    cube = lax.psum(cube_part, "depth")
    return 3.0 * square - 2.0 * cube


def dense_halves(upper, pattern, *tables):
    whole = dense(upper, pattern)
    depth = lax.axis_index("depth")
    return tuple(lax.dynamic_slice_in_dim(whole, at * MR, MR, 0) for at in (depth, 1 - depth))


def local(upper, pattern):
    *tables, fits = layout(pattern)
    mine, other = lax.cond(fits, sparse, dense_halves, upper, pattern, *tables)
    own = jnp.arange(2, dtype=jnp.int32) == lax.axis_index("depth")
    return jnp.where(own[:, None, None], mine[None], other[None]).reshape(upper.shape)


def solution(mesh):
    placed = (P("row", "col"), P())
    return jax.shard_map(
        local, mesh=mesh, in_specs=placed, out_specs=P("row", "col"), check_vma=False
    )
```

```python
import jax
import jax.numpy as jnp
from jax import lax
from jax.experimental import pallas as pl
from jax.experimental.pallas import tpu as pltpu
from jax.sharding import PartitionSpec as P

BS = 128
NB = 64
ROWS = 4
COLS = 16
NROW = 16
NCOL = 4
STRIPS = 16
PER = 44
CAP = 8 * PER
SRC = 3
HALF = 2
MR = HALF * BS
UNROLL = 8
VMEM = 62 * 1024 * 1024
ALL = ("row", "col", "depth")


def prefix(ones):
    ids = jnp.arange(NB, dtype=jnp.int32)
    before = (ids[:, None] < ids[None, :]).astype(jnp.float32)
    return jnp.dot(ones.astype(jnp.float32), before, preferred_element_type=jnp.float32).astype(jnp.int32)


def layout(pattern):
    ids = jnp.arange(NB, dtype=jnp.int32)
    stored = jnp.where(ids[:, None] < ids[None, :], pattern, 0) + (ids[:, None] == ids[None, :])
    stored = (stored != 0).astype(jnp.int32)
    local = stored.reshape(NROW, ROWS, NCOL, COLS).transpose(0, 2, 1, 3).reshape(NB, NB)
    rank = prefix(local)
    count = jnp.sum(local, axis=1)
    first = prefix(count[None, :])[0]
    last = first + count
    slot = (first[:, None] + rank).reshape(NROW, NCOL, ROWS, COLS).transpose(0, 2, 1, 3).reshape(NB, NB)
    fits = jnp.all(count <= 8 * SRC) & (last[NB - 1] <= CAP)
    return stored, slot, first, last, fits


def pack_kernel(here_ref, pattern_ref, pattern_vec, upper_ref, out_ref, list_ref, sem):
    row, col, depth = here_ref[0], here_ref[1], here_ref[2]
    i = lax.broadcasted_iota(jnp.int32, (NB, NB), 0)
    j = lax.broadcasted_iota(jnp.int32, (NB, NB), 1)
    stored = (i == j) | ((i < j) & (pattern_vec[...] != 0))
    earlier = (i // ROWS) * NCOL + j // COLS < row * NCOL + col
    first = jnp.sum(jnp.where(stored & earlier, 1.0, 0.0)).astype(jnp.int32)

    def copy(at):
        code = list_ref[at]
        a, b, n = code & 3, (code >> 2) & 15, code >> 6
        return pltpu.make_async_copy(
            upper_ref.at[pl.ds(a * STRIPS, STRIPS), :, pl.ds(pl.multiple_of(b * BS, BS), BS)],
            out_ref.at[:, ((first + n) >> 1) & 3, n >> 3],
            sem.at[at],
        )

    def find(a, state):
        def one(b, state):
            n, at = state
            i, j = row * ROWS + a, col * COLS + b
            there = (i == j) | ((i < j) & (pattern_ref[i, j] != 0))
            ours = there & (((first + n) & 1) == depth) & (n < 8 * SRC)

            @pl.when(ours)
            def _():
                list_ref[at] = a + 4 * b + 64 * n
                copy(at).start()

            return n + there.astype(jnp.int32), at + ours.astype(jnp.int32)

        return lax.fori_loop(0, COLS, one, state)

    _, found = lax.fori_loop(0, ROWS, find, (jnp.int32(0), jnp.int32(0)))

    def finish(at, _):
        copy(at).wait()
        code = list_ref[at]
        a, b, n = code & 3, (code >> 2) & 15, code >> 6

        @pl.when(row * ROWS + a == col * COLS + b)
        def _():
            z = ((first + n) >> 1) & 3
            x = out_ref[:, z, n >> 3].reshape(BS, BS)
            out_ref[:, z, n >> 3] = (0.5 * (x + x.T)).reshape(STRIPS, 8, BS)

        return 0

    lax.fori_loop(0, found, finish, 0)


def select_kernel(index_ref, got_ref, out_ref):
    for u in range(PER):
        out_ref[u] = got_ref[index_ref[u]]


def split(x):
    high = x.astype(jnp.bfloat16)
    return high, (x - high.astype(jnp.float32)).astype(jnp.bfloat16)


def main_kernel(sd_ref, sdn_ref, st_ref, stn_ref, pd_ref, pdn_ref, pt_ref, ptn_ref, row_ref, rn_ref, where_ref,
                blocks_hbm, out_ref, blocks_ref, a_ref, s_ref, sum_ref, cube_ref, item_ref, sem):
    first_col = where_ref[0]
    loads = [
        pltpu.make_async_copy(blocks_hbm.at[pl.ds(2 * i, 2)], blocks_ref.at[pl.ds(2 * i, 2)], sem.at[i])
        for i in range(STRIPS // 2)
    ]
    for load in loads:
        load.start()
    a_ref[...] = jnp.zeros_like(a_ref)
    sum_ref[...] = jnp.zeros_like(sum_ref)
    cube_ref[...] = jnp.zeros_like(cube_ref)
    s_ref[NB] = jnp.zeros((2 * MR, BS), jnp.bfloat16)

    def list_items(count_ref, columns, at):
        def column(k, n):
            def one(i, n):
                item_ref[at, n] = k * NB + 2 * i
                return n + 1

            return lax.fori_loop(0, (count_ref[k] + 1) >> 1, one, n)

        n = lax.fori_loop(0, columns, column, 0)
        for i in range(UNROLL - 1):
            item_ref[at, n + i] = columns * NB
        return (n + UNROLL - 1) // UNROLL

    def block(slot):
        return blocks_ref[:, slot & 7, slot >> 3].reshape(BS, BS)

    rounds = [list_items(sdn_ref, NB, 0), list_items(stn_ref, NB, 1), list_items(pdn_ref, COLS, 2), list_items(ptn_ref, COLS, 3)]
    for load in loads:
        load.wait()

    for h in range(HALF):
        def fill(p, _, h=h):
            code = row_ref[h, p]
            m = code & 127
            x = block((code >> 7) & 511)

            def put(x):
                high, low = split(x)
                a_ref[m, h * BS:(h + 1) * BS] = high
                a_ref[m, MR + h * BS:MR + (h + 1) * BS] = low

            @pl.when(code < 65536)
            def _():
                put(x)

            @pl.when(code >= 65536)
            def _():
                put(x.T)

            return 0

        lax.fori_loop(0, rn_ref[h], fill, 0)

    def product(left_ref, list_ref, mirrored, k, p):
        c0, c1 = list_ref[k, p], list_ref[k, p + 1]
        left = jnp.concatenate([left_ref[c0 & 127], left_ref[c1 & 127]], axis=1)
        h0, l0 = split(block(c0 >> 7))
        h1, l1 = split(block(c1 >> 7))
        if mirrored:
            right = jnp.concatenate([jnp.concatenate([h0, h1], axis=1), jnp.concatenate([l0, l1], axis=1)], axis=0)
            z = lax.dot_general(left, right, (((1,), (1,)), ((), ())), preferred_element_type=jnp.float32)
        else:
            right = jnp.concatenate([jnp.concatenate([h0, l0], axis=1), jnp.concatenate([h1, l1], axis=1)], axis=0)
            z = jnp.dot(left, right, preferred_element_type=jnp.float32)
        z = z[:MR] + z[MR:]
        return z[:, :BS] + z[:, BS:]

    def work(left_ref, list_ref, mirrored, into_ref, at):
        def several(i, _):
            items = [item_ref[at, UNROLL * i + e] for e in range(UNROLL)]
            done = [product(left_ref, list_ref, mirrored, item >> 6, item & 63) for item in items]
            for item, z in zip(items, done):
                into_ref[item >> 6] += z
            return 0

        lax.fori_loop(0, rounds[at], several, 0)

    work(a_ref, sd_ref, False, sum_ref, 0)
    work(a_ref, st_ref, True, sum_ref, 1)

    def halves(k, _):
        high, low = split(sum_ref[k])
        s_ref[k, :MR] = high
        s_ref[k, MR:] = low
        return 0

    lax.fori_loop(0, NB, halves, 0, unroll=2)
    work(s_ref, pd_ref, False, cube_ref, 2)
    work(s_ref, pt_ref, True, cube_ref, 3)
    for j in range(COLS):
        out_ref[:, j * BS:(j + 1) * BS] = 3.0 * sum_ref[first_col + j] - 2.0 * cube_ref[j]


def compact(chosen, codes, pad):
    ids = jnp.arange(NB, dtype=jnp.int32)
    at = jnp.where(chosen, prefix(chosen), -1)
    hit = at[:, :, None] == ids[None, None, :]
    table = pad + jnp.sum(jnp.where(hit, (codes - pad)[:, :, None], 0), axis=1)
    return jnp.pad(table, ((0, 1), (0, 0)), constant_values=pad)


def count(chosen):
    return jnp.sum(chosen.astype(jnp.int32), axis=1)


SMEM = pl.BlockSpec(memory_space=pltpu.SMEM)
INVMEM = pl.BlockSpec(memory_space=pltpu.VMEM)
ANY = pl.BlockSpec(memory_space=pl.ANY)


def gather(upper, pattern, first, last):
    ids = jnp.arange(NB, dtype=jnp.int32)
    row, col, depth = lax.axis_index("row"), lax.axis_index("col"), lax.axis_index("depth")
    packed = pl.pallas_call(
        pack_kernel,
        out_shape=jax.ShapeDtypeStruct((STRIPS, NCOL, SRC, 8, BS), jnp.float32),
        in_specs=[SMEM, SMEM, INVMEM, ANY],
        out_specs=INVMEM,
        scratch_shapes=[pltpu.SMEM((8 * SRC,), jnp.int32), pltpu.SemaphoreType.DMA((8 * SRC,))],
        compiler_params=pltpu.CompilerParams(vmem_limit_bytes=16 * 1024 * 1024),
    )(jnp.stack([row, col, depth]).astype(jnp.int32), pattern, pattern, upper.reshape(ROWS * STRIPS, 8, COLS * BS))
    got = lax.all_to_all(packed.reshape(NB, SRC * 8, BS), ("row", "col"), 0, 0, tiled=True)
    g = 8 * jnp.arange(PER, dtype=jnp.int32) + 2 * col + depth
    source = jnp.minimum(jnp.sum((last[None, :] <= g[:, None]).astype(jnp.int32), axis=1), NB - 1)
    source_first = jnp.sum(jnp.where(source[:, None] == ids[None, :], first[None, :], 0), axis=1)
    pick = source * SRC + jnp.clip((g - source_first) >> 3, 0, SRC - 1)
    share = pl.pallas_call(
        select_kernel,
        out_shape=jax.ShapeDtypeStruct((PER, 8, BS), jnp.float32),
        in_specs=[SMEM, INVMEM],
        out_specs=INVMEM,
        compiler_params=pltpu.CompilerParams(vmem_limit_bytes=16 * 1024 * 1024),
    )(pick, got.reshape(NB * SRC, 8, BS))
    return lax.all_gather(share, ALL, axis=0).reshape(STRIPS, 8, PER, 8, BS)


def work_lists(stored, slot):
    ids = jnp.arange(NB, dtype=jnp.int32)
    row, col, depth = lax.axis_index("row"), lax.axis_index("col"), lax.axis_index("depth")
    below = ids[:, None] > ids[None, :]
    both = jnp.where(below, stored.T, stored) != 0
    slots = jnp.where(below, slot.T, slot)
    codes = ids[None, :] + BS * slots
    my_row = row * ROWS + depth * HALF
    near = jnp.any(lax.dynamic_slice_in_dim(both, my_row, HALF, 0), axis=0)
    direct = both & (ids[None, :] <= ids[:, None])
    mirrored = both & (ids[None, :] > ids[:, None])
    sd, st = direct & near[None, :], mirrored & near[None, :]
    col_direct = lax.dynamic_slice_in_dim(direct, col * COLS, COLS, 0)
    col_mirrored = lax.dynamic_slice_in_dim(mirrored, col * COLS, COLS, 0)
    col_codes = lax.dynamic_slice_in_dim(codes, col * COLS, COLS, 0)
    row_both = lax.dynamic_slice_in_dim(both, my_row, HALF, 0)
    row_codes = lax.dynamic_slice_in_dim(codes + 65536 * below, my_row, HALF, 0)
    return (
        compact(sd, codes, NB), count(sd), compact(st, codes, NB), count(st),
        compact(col_direct, col_codes, NB), count(col_direct), compact(col_mirrored, col_codes, NB), count(col_mirrored),
        compact(row_both, row_codes, NB), count(row_both), (col * COLS)[None].astype(jnp.int32),
    )


def multiply(upper, pattern, blocks, *lists):
    return pl.pallas_call(
        main_kernel,
        out_shape=jax.ShapeDtypeStruct((MR, COLS * BS), jnp.float32),
        in_specs=[SMEM] * 11 + [ANY],
        out_specs=INVMEM,
        scratch_shapes=[
            pltpu.VMEM((STRIPS, 8, PER, 8, BS), jnp.float32),
            pltpu.VMEM((NB + 1, 2 * MR, BS), jnp.bfloat16),
            pltpu.VMEM((NB + 1, 2 * MR, BS), jnp.bfloat16),
            pltpu.VMEM((NB + 1, MR, BS), jnp.float32),
            pltpu.VMEM((COLS + 1, MR, BS), jnp.float32),
            pltpu.SMEM((4, NB * NB // 2 + NB + UNROLL), jnp.int32),
            pltpu.SemaphoreType.DMA((STRIPS // 2,)),
        ],
        compiler_params=pltpu.CompilerParams(vmem_limit_bytes=VMEM),
    )(*lists, blocks)


def join_kernel(depth_ref, mine_ref, other_ref, out_ref, sem):
    depth = depth_ref[0]
    copies = []
    for k, (part_ref, half) in enumerate(((mine_ref, depth), (other_ref, 1 - depth))):
        for i in range(4):
            rows = MR // 4
            to = pl.multiple_of(half * MR + i * rows, rows)
            copies.append(pltpu.make_async_copy(part_ref.at[pl.ds(i * rows, rows)], out_ref.at[pl.ds(to, rows)], sem.at[k, i]))
    for copy in copies:
        copy.start()
    for copy in copies:
        copy.wait()


def dense(upper, pattern):
    rows_tile, cols_tile = upper.shape
    nrow = lax.axis_size("row")
    ncol = lax.axis_size("col")
    ndep = lax.axis_size("depth")
    row_blocks = rows_tile // BS
    col_blocks = cols_tile // BS
    spread = upper.reshape(row_blocks, ncol, BS // ncol, col_blocks, nrow, BS // nrow)
    spread = spread.transpose(4, 1, 0, 2, 3, 5).reshape(
        nrow * ncol, row_blocks, BS // ncol, col_blocks, BS // nrow
    )
    spread = lax.all_to_all(spread, ("row", "col"), split_axis=0, concat_axis=0, tiled=True)
    spread = spread.reshape(nrow, ncol, row_blocks, BS // ncol, col_blocks, BS // nrow)
    spread = spread.transpose(0, 2, 3, 1, 4, 5).reshape(
        ncol, col_blocks, BS // ncol, nrow, row_blocks, BS // nrow
    )
    spread = spread.transpose(3, 0, 4, 5, 1, 2).reshape(
        nrow * ncol, row_blocks, BS // nrow, col_blocks, BS // ncol
    )
    spread = lax.all_to_all(spread, ("row", "col"), split_axis=0, concat_axis=0, tiled=True)
    spread = spread.reshape(nrow, ncol, row_blocks, BS // nrow, col_blocks, BS // ncol)
    mirror = spread.transpose(2, 0, 3, 4, 1, 5).reshape(row_blocks, BS, col_blocks, BS)
    row_index = lax.axis_index("row")
    col_index = lax.axis_index("col")
    row_first = row_index * row_blocks
    col_first = col_index * col_blocks
    global_rows = row_first + jnp.arange(row_blocks, dtype=jnp.int32)
    global_cols = col_first + jnp.arange(col_blocks, dtype=jnp.int32)
    above = global_rows[:, None] < global_cols[None, :]
    below = global_rows[:, None] > global_cols[None, :]
    upper_pat = lax.dynamic_slice(pattern, (row_first, col_first), (row_blocks, col_blocks))
    lower_pat = lax.dynamic_slice(pattern, (col_first, row_first), (col_blocks, row_blocks)).T
    keep = jnp.where(above, upper_pat, jnp.where(below, lower_pat, 1)).astype(jnp.float32)
    own = upper.reshape(row_blocks, BS, col_blocks, BS)
    blended = jnp.where(
        above[:, None, :, None],
        own,
        jnp.where(below[:, None, :, None], mirror, 0.5 * (own + mirror)),
    )
    density = (blended * keep[:, None, :, None]).reshape(rows_tile, cols_tile)
    layer = lax.axis_index("depth")

    def layer_columns(tile):
        split = tile.reshape(rows_tile, col_blocks // ndep, ndep, BS)
        return lax.dynamic_slice_in_dim(split, layer, 1, 2).reshape(
            rows_tile, col_blocks // ndep * BS
        )

    split_rows = density.reshape(row_blocks // ndep, ndep, BS, cols_tile)
    layer_rows = lax.dynamic_slice_in_dim(split_rows, layer, 1, 1).reshape(
        row_blocks // ndep * BS, cols_tile
    )
    panel = lax.all_gather(layer_rows, "row", axis=0, tiled=True)

    def accumulate(piece):
        return jnp.dot(
            piece, panel, precision=lax.Precision.HIGHEST, preferred_element_type=jnp.float32
        )

    square_part = accumulate(lax.all_gather(layer_columns(density), "col", axis=1, tiled=True))
    square = lax.psum(square_part, "depth")
    cube_part = accumulate(lax.all_gather(layer_columns(square), "col", axis=1, tiled=True))
    cube = lax.psum(cube_part, "depth")
    return 3.0 * square - 2.0 * cube


def dense_half(upper, pattern, *rest):
    return lax.dynamic_slice_in_dim(dense(upper, pattern), lax.axis_index("depth") * MR, MR, 0)


def local(upper, pattern):
    stored, slot, first, last, fits = layout(pattern)
    blocks = gather(upper, pattern, first, last)
    lists = lax.optimization_barrier(work_lists(stored, slot))
    mine = lax.cond(fits, multiply, dense_half, upper, pattern, blocks, *lists)
    other = lax.ppermute(mine, "depth", [(0, 1), (1, 0)])
    return pl.pallas_call(
        join_kernel,
        out_shape=jax.ShapeDtypeStruct(upper.shape, jnp.float32),
        in_specs=[SMEM, ANY, ANY],
        out_specs=ANY,
        scratch_shapes=[pltpu.SemaphoreType.DMA((2, 4))],
        compiler_params=pltpu.CompilerParams(vmem_limit_bytes=16 * 1024 * 1024),
    )(lax.axis_index("depth")[None].astype(jnp.int32), mine, other)


def solution(mesh):
    placed = (P("row", "col"), P())
    return jax.shard_map(
        local, mesh=mesh, in_specs=placed, out_specs=P("row", "col"), check_vma=False
    )
```

```python
import jax
import jax.numpy as jnp
from jax import lax
from jax.experimental import pallas as pl
from jax.experimental.pallas import tpu as pltpu
from jax.sharding import PartitionSpec as P

BS = 128
NB = 64
ROWS = 4
COLS = 16
NROW = 16
NCOL = 4
STRIPS = 16
PER = 44
CAP = 8 * PER
SRC = 3
HALF = 2
MR = HALF * BS
UNROLL = 8
VMEM = 62 * 1024 * 1024
ALL = ("row", "col", "depth")


def prefix(ones):
    ids = jnp.arange(NB, dtype=jnp.int32)
    before = (ids[:, None] < ids[None, :]).astype(jnp.float32)
    return jnp.dot(ones.astype(jnp.float32), before, preferred_element_type=jnp.float32).astype(jnp.int32)


def layout(pattern):
    ids = jnp.arange(NB, dtype=jnp.int32)
    stored = jnp.where(ids[:, None] < ids[None, :], pattern, 0) + (ids[:, None] == ids[None, :])
    stored = (stored != 0).astype(jnp.int32)
    local = stored.reshape(NROW, ROWS, NCOL, COLS).transpose(0, 2, 1, 3).reshape(NB, NB)
    rank = prefix(local)
    count = jnp.sum(local, axis=1)
    first = prefix(count[None, :])[0]
    last = first + count
    slot = (first[:, None] + rank).reshape(NROW, NCOL, ROWS, COLS).transpose(0, 2, 1, 3).reshape(NB, NB)
    fits = jnp.all(count <= 8 * SRC) & (last[NB - 1] <= CAP)
    return stored, slot, first, last, fits


def pack_kernel(here_ref, pattern_ref, pattern_vec, upper_ref, out_ref, list_ref, sem):
    row, col, depth = here_ref[0], here_ref[1], here_ref[2]
    i = lax.broadcasted_iota(jnp.int32, (NB, NB), 0)
    j = lax.broadcasted_iota(jnp.int32, (NB, NB), 1)
    stored = (i == j) | ((i < j) & (pattern_vec[...] != 0))
    earlier = (i // ROWS) * NCOL + j // COLS < row * NCOL + col
    first = jnp.sum(jnp.where(stored & earlier, 1.0, 0.0)).astype(jnp.int32)

    def copy(at):
        code = list_ref[at]
        a, b, n = code & 3, (code >> 2) & 15, code >> 6
        return pltpu.make_async_copy(
            upper_ref.at[pl.ds(a * STRIPS, STRIPS), :, pl.ds(pl.multiple_of(b * BS, BS), BS)],
            out_ref.at[:, ((first + n) >> 1) & 3, n >> 3],
            sem.at[at],
        )

    def find(a, state):
        def one(b, state):
            n, at = state
            i, j = row * ROWS + a, col * COLS + b
            there = (i == j) | ((i < j) & (pattern_ref[i, j] != 0))
            ours = there & (((first + n) & 1) == depth) & (n < 8 * SRC)

            @pl.when(ours)
            def _():
                list_ref[at] = a + 4 * b + 64 * n
                copy(at).start()

            return n + there.astype(jnp.int32), at + ours.astype(jnp.int32)

        return lax.fori_loop(0, COLS, one, state)

    _, found = lax.fori_loop(0, ROWS, find, (jnp.int32(0), jnp.int32(0)))

    def finish(at, _):
        copy(at).wait()
        code = list_ref[at]
        a, b, n = code & 3, (code >> 2) & 15, code >> 6

        @pl.when(row * ROWS + a == col * COLS + b)
        def _():
            z = ((first + n) >> 1) & 3
            x = out_ref[:, z, n >> 3].reshape(BS, BS)
            out_ref[:, z, n >> 3] = (0.5 * (x + x.T)).reshape(STRIPS, 8, BS)

        return 0

    lax.fori_loop(0, found, finish, 0)


def select_kernel(index_ref, got_ref, out_ref):
    for u in range(PER):
        out_ref[u] = got_ref[index_ref[u]]


def split(x):
    high = x.astype(jnp.bfloat16)
    return high, (x - high.astype(jnp.float32)).astype(jnp.bfloat16)


def main_kernel(sd_ref, sdn_ref, st_ref, stn_ref, pd_ref, pdn_ref, pt_ref, ptn_ref, row_ref, rn_ref, where_ref,
                blocks_hbm, out_ref, blocks_ref, a_ref, s_ref, sum_ref, cube_ref, item_ref, sem):
    first_col = where_ref[0]
    loads = [
        pltpu.make_async_copy(blocks_hbm.at[pl.ds(2 * i, 2)], blocks_ref.at[pl.ds(2 * i, 2)], sem.at[i])
        for i in range(STRIPS // 2)
    ]
    for load in loads:
        load.start()
    a_ref[...] = jnp.zeros_like(a_ref)
    sum_ref[...] = jnp.zeros_like(sum_ref)
    cube_ref[...] = jnp.zeros_like(cube_ref)
    s_ref[NB] = jnp.zeros((2 * MR, BS), jnp.bfloat16)

    def list_items(count_ref, columns, at):
        def column(k, n):
            def one(i, n):
                item_ref[at, n] = k * NB + 2 * i
                return n + 1

            return lax.fori_loop(0, (count_ref[k] + 1) >> 1, one, n)

        n = lax.fori_loop(0, columns, column, 0)
        for i in range(UNROLL - 1):
            item_ref[at, n + i] = columns * NB
        return (n + UNROLL - 1) // UNROLL

    def block(slot):
        return blocks_ref[:, slot & 7, slot >> 3].reshape(BS, BS)

    rounds = [list_items(sdn_ref, NB, 0), list_items(stn_ref, NB, 1), list_items(pdn_ref, COLS, 2), list_items(ptn_ref, COLS, 3)]
    for load in loads:
        load.wait()

    for h in range(HALF):
        def fill(p, _, h=h):
            code = row_ref[h, p]
            m = code & 127
            x = block((code >> 7) & 511)

            def put(x):
                high, low = split(x)
                a_ref[m, h * BS:(h + 1) * BS] = high
                a_ref[m, MR + h * BS:MR + (h + 1) * BS] = low

            @pl.when(code < 65536)
            def _():
                put(x)

            @pl.when(code >= 65536)
            def _():
                put(x.T)

            return 0

        lax.fori_loop(0, rn_ref[h], fill, 0)

    def product(left_ref, list_ref, mirrored, k, p):
        c0, c1 = list_ref[k, p], list_ref[k, p + 1]
        left = jnp.concatenate([left_ref[c0 & 127], left_ref[c1 & 127]], axis=1)
        h0, l0 = split(block(c0 >> 7))
        h1, l1 = split(block(c1 >> 7))
        if mirrored:
            right = jnp.concatenate([jnp.concatenate([h0, h1], axis=1), jnp.concatenate([l0, l1], axis=1)], axis=0)
            z = lax.dot_general(left, right, (((1,), (1,)), ((), ())), preferred_element_type=jnp.float32)
        else:
            right = jnp.concatenate([jnp.concatenate([h0, l0], axis=1), jnp.concatenate([h1, l1], axis=1)], axis=0)
            z = jnp.dot(left, right, preferred_element_type=jnp.float32)
        z = z[:MR] + z[MR:]
        return z[:, :BS] + z[:, BS:]

    def work(left_ref, list_ref, mirrored, into_ref, at):
        def several(i, _):
            items = [item_ref[at, UNROLL * i + e] for e in range(UNROLL)]
            done = [product(left_ref, list_ref, mirrored, item >> 6, item & 63) for item in items]
            for item, z in zip(items, done):
                into_ref[item >> 6] += z
            return 0

        lax.fori_loop(0, rounds[at], several, 0)

    work(a_ref, sd_ref, False, sum_ref, 0)
    work(a_ref, st_ref, True, sum_ref, 1)

    def halves(k, _):
        high, low = split(sum_ref[k])
        s_ref[k, :MR] = high
        s_ref[k, MR:] = low
        return 0

    lax.fori_loop(0, NB, halves, 0, unroll=2)
    work(s_ref, pd_ref, False, cube_ref, 2)
    work(s_ref, pt_ref, True, cube_ref, 3)
    for j in range(COLS):
        out_ref[:, j * BS:(j + 1) * BS] = 3.0 * sum_ref[first_col + j] - 2.0 * cube_ref[j]


def compact(chosen, codes, pad):
    ids = jnp.arange(NB, dtype=jnp.int32)
    at = jnp.where(chosen, prefix(chosen), -1)
    hit = at[:, :, None] == ids[None, None, :]
    table = pad + jnp.sum(jnp.where(hit, (codes - pad)[:, :, None], 0), axis=1)
    return jnp.pad(table, ((0, 1), (0, 0)), constant_values=pad)


def count(chosen):
    return jnp.sum(chosen.astype(jnp.int32), axis=1)


SMEM = pl.BlockSpec(memory_space=pltpu.SMEM)
INVMEM = pl.BlockSpec(memory_space=pltpu.VMEM)
ANY = pl.BlockSpec(memory_space=pl.ANY)


def gather(upper, pattern, first, last):
    ids = jnp.arange(NB, dtype=jnp.int32)
    row, col, depth = lax.axis_index("row"), lax.axis_index("col"), lax.axis_index("depth")
    packed = pl.pallas_call(
        pack_kernel,
        out_shape=jax.ShapeDtypeStruct((STRIPS, NCOL, SRC, 8, BS), jnp.float32),
        in_specs=[SMEM, SMEM, INVMEM, ANY],
        out_specs=INVMEM,
        scratch_shapes=[pltpu.SMEM((8 * SRC,), jnp.int32), pltpu.SemaphoreType.DMA((8 * SRC,))],
        compiler_params=pltpu.CompilerParams(vmem_limit_bytes=16 * 1024 * 1024),
    )(jnp.stack([row, col, depth]).astype(jnp.int32), pattern, pattern, upper.reshape(ROWS * STRIPS, 8, COLS * BS))
    got = lax.all_to_all(packed.reshape(NB, SRC * 8, BS), ("row", "col"), 0, 0, tiled=True)
    g = 8 * jnp.arange(PER, dtype=jnp.int32) + 2 * col + depth
    source = jnp.minimum(jnp.sum((last[None, :] <= g[:, None]).astype(jnp.int32), axis=1), NB - 1)
    source_first = jnp.sum(jnp.where(source[:, None] == ids[None, :], first[None, :], 0), axis=1)
    pick = source * SRC + jnp.clip((g - source_first) >> 3, 0, SRC - 1)
    share = pl.pallas_call(
        select_kernel,
        out_shape=jax.ShapeDtypeStruct((PER, 8, BS), jnp.float32),
        in_specs=[SMEM, INVMEM],
        out_specs=INVMEM,
        compiler_params=pltpu.CompilerParams(vmem_limit_bytes=16 * 1024 * 1024),
    )(pick, got.reshape(NB * SRC, 8, BS))
    return lax.all_gather(share, ALL, axis=0).reshape(STRIPS, 8, PER, 8, BS)


def work_lists(stored, slot):
    ids = jnp.arange(NB, dtype=jnp.int32)
    row, col, depth = lax.axis_index("row"), lax.axis_index("col"), lax.axis_index("depth")
    below = ids[:, None] > ids[None, :]
    both = jnp.where(below, stored.T, stored) != 0
    slots = jnp.where(below, slot.T, slot)
    codes = ids[None, :] + BS * slots
    my_row = row * ROWS + depth * HALF
    near = jnp.any(lax.dynamic_slice_in_dim(both, my_row, HALF, 0), axis=0)
    direct = both & (ids[None, :] <= ids[:, None])
    mirrored = both & (ids[None, :] > ids[:, None])
    sd, st = direct & near[None, :], mirrored & near[None, :]
    col_direct = lax.dynamic_slice_in_dim(direct, col * COLS, COLS, 0)
    col_mirrored = lax.dynamic_slice_in_dim(mirrored, col * COLS, COLS, 0)
    col_codes = lax.dynamic_slice_in_dim(codes, col * COLS, COLS, 0)
    row_both = lax.dynamic_slice_in_dim(both, my_row, HALF, 0)
    row_codes = lax.dynamic_slice_in_dim(codes + 65536 * below, my_row, HALF, 0)
    return (
        compact(sd, codes, NB), count(sd), compact(st, codes, NB), count(st),
        compact(col_direct, col_codes, NB), count(col_direct), compact(col_mirrored, col_codes, NB), count(col_mirrored),
        compact(row_both, row_codes, NB), count(row_both), (col * COLS)[None].astype(jnp.int32),
    )


def multiply(upper, pattern, blocks, *lists):
    return pl.pallas_call(
        main_kernel,
        out_shape=jax.ShapeDtypeStruct((MR, COLS * BS), jnp.float32),
        in_specs=[SMEM] * 11 + [ANY],
        out_specs=INVMEM,
        scratch_shapes=[
            pltpu.VMEM((STRIPS, 8, PER, 8, BS), jnp.float32),
            pltpu.VMEM((NB + 1, 2 * MR, BS), jnp.bfloat16),
            pltpu.VMEM((NB + 1, 2 * MR, BS), jnp.bfloat16),
            pltpu.VMEM((NB + 1, MR, BS), jnp.float32),
            pltpu.VMEM((COLS + 1, MR, BS), jnp.float32),
            pltpu.SMEM((4, NB * NB // 2 + NB + UNROLL), jnp.int32),
            pltpu.SemaphoreType.DMA((STRIPS // 2,)),
        ],
        compiler_params=pltpu.CompilerParams(vmem_limit_bytes=VMEM),
    )(*lists, blocks)


def join_kernel(depth_ref, mine_ref, other_ref, out_ref, held_ref, in_sem, out_sem):
    depth = depth_ref[0]
    rows = MR // 4
    loads, stores = [], []
    for i in range(8):
        part_ref, half = ((mine_ref, depth), (other_ref, 1 - depth))[i % 2]
        at = i // 2 * rows
        to = pl.multiple_of(half * MR + at, rows)
        loads.append(pltpu.make_async_copy(part_ref.at[pl.ds(at, rows)], held_ref.at[i], in_sem.at[i]))
        stores.append(pltpu.make_async_copy(held_ref.at[i], out_ref.at[pl.ds(to, rows)], out_sem.at[i]))
    for load in loads:
        load.start()
    for load, store in zip(loads, stores):
        load.wait()
        store.start()
    for store in stores:
        store.wait()


def dense(upper, pattern):
    rows_tile, cols_tile = upper.shape
    nrow = lax.axis_size("row")
    ncol = lax.axis_size("col")
    ndep = lax.axis_size("depth")
    row_blocks = rows_tile // BS
    col_blocks = cols_tile // BS
    spread = upper.reshape(row_blocks, ncol, BS // ncol, col_blocks, nrow, BS // nrow)
    spread = spread.transpose(4, 1, 0, 2, 3, 5).reshape(
        nrow * ncol, row_blocks, BS // ncol, col_blocks, BS // nrow
    )
    spread = lax.all_to_all(spread, ("row", "col"), split_axis=0, concat_axis=0, tiled=True)
    spread = spread.reshape(nrow, ncol, row_blocks, BS // ncol, col_blocks, BS // nrow)
    spread = spread.transpose(0, 2, 3, 1, 4, 5).reshape(
        ncol, col_blocks, BS // ncol, nrow, row_blocks, BS // nrow
    )
    spread = spread.transpose(3, 0, 4, 5, 1, 2).reshape(
        nrow * ncol, row_blocks, BS // nrow, col_blocks, BS // ncol
    )
    spread = lax.all_to_all(spread, ("row", "col"), split_axis=0, concat_axis=0, tiled=True)
    spread = spread.reshape(nrow, ncol, row_blocks, BS // nrow, col_blocks, BS // ncol)
    mirror = spread.transpose(2, 0, 3, 4, 1, 5).reshape(row_blocks, BS, col_blocks, BS)
    row_index = lax.axis_index("row")
    col_index = lax.axis_index("col")
    row_first = row_index * row_blocks
    col_first = col_index * col_blocks
    global_rows = row_first + jnp.arange(row_blocks, dtype=jnp.int32)
    global_cols = col_first + jnp.arange(col_blocks, dtype=jnp.int32)
    above = global_rows[:, None] < global_cols[None, :]
    below = global_rows[:, None] > global_cols[None, :]
    upper_pat = lax.dynamic_slice(pattern, (row_first, col_first), (row_blocks, col_blocks))
    lower_pat = lax.dynamic_slice(pattern, (col_first, row_first), (col_blocks, row_blocks)).T
    keep = jnp.where(above, upper_pat, jnp.where(below, lower_pat, 1)).astype(jnp.float32)
    own = upper.reshape(row_blocks, BS, col_blocks, BS)
    blended = jnp.where(
        above[:, None, :, None],
        own,
        jnp.where(below[:, None, :, None], mirror, 0.5 * (own + mirror)),
    )
    density = (blended * keep[:, None, :, None]).reshape(rows_tile, cols_tile)
    layer = lax.axis_index("depth")

    def layer_columns(tile):
        split = tile.reshape(rows_tile, col_blocks // ndep, ndep, BS)
        return lax.dynamic_slice_in_dim(split, layer, 1, 2).reshape(
            rows_tile, col_blocks // ndep * BS
        )

    split_rows = density.reshape(row_blocks // ndep, ndep, BS, cols_tile)
    layer_rows = lax.dynamic_slice_in_dim(split_rows, layer, 1, 1).reshape(
        row_blocks // ndep * BS, cols_tile
    )
    panel = lax.all_gather(layer_rows, "row", axis=0, tiled=True)

    def accumulate(piece):
        return jnp.dot(
            piece, panel, precision=lax.Precision.HIGHEST, preferred_element_type=jnp.float32
        )

    square_part = accumulate(lax.all_gather(layer_columns(density), "col", axis=1, tiled=True))
    square = lax.psum(square_part, "depth")
    cube_part = accumulate(lax.all_gather(layer_columns(square), "col", axis=1, tiled=True))
    cube = lax.psum(cube_part, "depth")
    return 3.0 * square - 2.0 * cube


def dense_half(upper, pattern, *rest):
    return lax.dynamic_slice_in_dim(dense(upper, pattern), lax.axis_index("depth") * MR, MR, 0)


def local(upper, pattern):
    stored, slot, first, last, fits = layout(pattern)
    blocks = gather(upper, pattern, first, last)
    lists = lax.optimization_barrier(work_lists(stored, slot))
    mine = lax.cond(fits, multiply, dense_half, upper, pattern, blocks, *lists)
    other = lax.ppermute(mine, "depth", [(0, 1), (1, 0)])
    return pl.pallas_call(
        join_kernel,
        out_shape=jax.ShapeDtypeStruct(upper.shape, jnp.float32),
        in_specs=[SMEM, ANY, ANY],
        out_specs=ANY,
        scratch_shapes=[
            pltpu.VMEM((8, MR // 4, COLS * BS), jnp.float32),
            pltpu.SemaphoreType.DMA((8,)),
            pltpu.SemaphoreType.DMA((8,)),
        ],
        compiler_params=pltpu.CompilerParams(vmem_limit_bytes=16 * 1024 * 1024),
    )(lax.axis_index("depth")[None].astype(jnp.int32), mine, other)


def solution(mesh):
    placed = (P("row", "col"), P())
    return jax.shard_map(
        local, mesh=mesh, in_specs=placed, out_specs=P("row", "col"), check_vma=False
    )
```

```python
import jax
import jax.numpy as jnp
from jax import lax
from jax.experimental import pallas as pl
from jax.experimental.pallas import tpu as pltpu
from jax.sharding import PartitionSpec as P

BS = 128
NB = 64
ROWS = 4
COLS = 16
NROW = 16
NCOL = 4
STRIPS = 16
PER = 44
PARTS = 4
PART = PER // PARTS
ITEMS = 256
CAP = 8 * PER
SRC = 3
HALF = 2
MR = HALF * BS
UNROLL = 12
VMEM = 62 * 1024 * 1024
ALL = ("row", "col", "depth")


def prefix(ones):
    ids = jnp.arange(NB, dtype=jnp.int32)
    before = (ids[:, None] < ids[None, :]).astype(jnp.float32)
    return jnp.dot(ones.astype(jnp.float32), before, preferred_element_type=jnp.float32).astype(jnp.int32)


def layout(pattern):
    ids = jnp.arange(NB, dtype=jnp.int32)
    stored = jnp.where(ids[:, None] < ids[None, :], pattern, 0) + (ids[:, None] == ids[None, :])
    stored = (stored != 0).astype(jnp.int32)
    local = stored.reshape(NROW, ROWS, NCOL, COLS).transpose(0, 2, 1, 3).reshape(NB, NB)
    rank = prefix(local)
    count = jnp.sum(local, axis=1)
    first = prefix(count[None, :])[0]
    last = first + count
    slot = (first[:, None] + rank).reshape(NROW, NCOL, ROWS, COLS).transpose(0, 2, 1, 3).reshape(NB, NB)
    fits = jnp.all(count <= 8 * SRC) & (last[NB - 1] <= CAP)
    return stored, slot, first, last, fits


def pack_kernel(here_ref, pattern_ref, pattern_vec, upper_ref, out_ref, list_ref, sem):
    row, col, depth = here_ref[0], here_ref[1], here_ref[2]
    i = lax.broadcasted_iota(jnp.int32, (NB, NB), 0)
    j = lax.broadcasted_iota(jnp.int32, (NB, NB), 1)
    stored = (i == j) | ((i < j) & (pattern_vec[...] != 0))
    earlier = (i // ROWS) * NCOL + j // COLS < row * NCOL + col
    first = jnp.sum(jnp.where(stored & earlier, 1.0, 0.0)).astype(jnp.int32)

    def copy(at):
        code = list_ref[at]
        a, b, n = code & 3, (code >> 2) & 15, code >> 6
        return pltpu.make_async_copy(
            upper_ref.at[pl.ds(a * STRIPS, STRIPS), :, pl.ds(pl.multiple_of(b * BS, BS), BS)],
            out_ref.at[:, ((first + n) >> 1) & 3, n >> 3],
            sem.at[at],
        )

    def find(a, state):
        def one(b, state):
            n, at = state
            i, j = row * ROWS + a, col * COLS + b
            there = (i == j) | ((i < j) & (pattern_ref[i, j] != 0))
            ours = there & (((first + n) & 1) == depth) & (n < 8 * SRC)

            @pl.when(ours)
            def _():
                list_ref[at] = a + 4 * b + 64 * n
                copy(at).start()

            return n + there.astype(jnp.int32), at + ours.astype(jnp.int32)

        return lax.fori_loop(0, COLS, one, state, unroll=4)

    _, found = lax.fori_loop(0, ROWS, find, (jnp.int32(0), jnp.int32(0)))

    def finish(at, _):
        copy(at).wait()
        code = list_ref[at]
        a, b, n = code & 3, (code >> 2) & 15, code >> 6

        @pl.when(row * ROWS + a == col * COLS + b)
        def _():
            z = ((first + n) >> 1) & 3
            x = out_ref[:, z, n >> 3].reshape(BS, BS)
            out_ref[:, z, n >> 3] = (0.5 * (x + x.T)).reshape(STRIPS, 8, BS)

        return 0

    lax.fori_loop(0, found, finish, 0)


def select_kernel(index_ref, got_ref, out_ref):
    for u in range(PER):
        out_ref[u] = got_ref[index_ref[u]]


def split(x):
    high = x.astype(jnp.bfloat16)
    return high, (x - high.astype(jnp.float32)).astype(jnp.bfloat16)


def main_kernel(sd_ref, st_ref, pd_ref, pt_ref, item_ref, limit_ref, row_ref, rn_ref, where_ref,
                blocks_hbm, out_ref, blocks_ref, a_ref, s_ref, sum_ref, cube_ref, sem, row_sem):
    first_col = where_ref[0]

    def row_load(h, p, n):
        slot = (row_ref[h, p] >> 7) & 511
        return pltpu.make_async_copy(
            blocks_hbm.at[:, slot & 7, slot >> 3], sum_ref.at[n >> 1, pl.ds((n & 1) * STRIPS, STRIPS)], row_sem.at[n]
        )

    for h in range(HALF):
        def start(p, _, h=h):
            row_load(h, p, h * NB + p).start()
            return 0

        lax.fori_loop(0, rn_ref[h], start, 0)
    loads = [
        pltpu.make_async_copy(
            blocks_hbm.at[:, :, pl.ds(i * PART, PART)], blocks_ref.at[:, :, pl.ds(i * PART, PART)], sem.at[i]
        )
        for i in range(PARTS)
    ]
    for load in loads:
        load.start()
    a_ref[...] = jnp.zeros_like(a_ref)
    cube_ref[...] = jnp.zeros_like(cube_ref)
    s_ref[NB] = jnp.zeros((2 * MR, BS), jnp.bfloat16)

    def block(slot):
        return blocks_ref[:, slot & 7, slot >> 3].reshape(BS, BS)

    for h in range(HALF):
        def fill(p, _, h=h):
            code = row_ref[h, p]
            m = code & 127
            n = h * NB + p
            row_load(h, p, n).wait()
            x = sum_ref[n >> 1, pl.ds((n & 1) * STRIPS, STRIPS)].reshape(BS, BS)

            def put(x):
                high, low = split(x)
                a_ref[m, h * BS:(h + 1) * BS] = high
                a_ref[m, MR + h * BS:MR + (h + 1) * BS] = low

            @pl.when(code < 65536)
            def _():
                put(x)

            @pl.when(code >= 65536)
            def _():
                put(x.T)

            return 0

        lax.fori_loop(0, rn_ref[h], fill, 0)
    sum_ref[...] = jnp.zeros_like(sum_ref)

    def product(left_ref, list_ref, mirrored, k, p):
        c0, c1 = list_ref[k, p], list_ref[k, p + 1]
        left = jnp.concatenate([left_ref[c0 & 127], left_ref[c1 & 127]], axis=1)
        h0, l0 = split(block(c0 >> 7))
        h1, l1 = split(block(c1 >> 7))
        if mirrored:
            right = jnp.concatenate([jnp.concatenate([h0, h1], axis=1), jnp.concatenate([l0, l1], axis=1)], axis=0)
            z = lax.dot_general(left, right, (((1,), (1,)), ((), ())), preferred_element_type=jnp.float32)
        else:
            right = jnp.concatenate([jnp.concatenate([h0, l0], axis=1), jnp.concatenate([h1, l1], axis=1)], axis=0)
            z = jnp.dot(left, right, preferred_element_type=jnp.float32)
        z = z[:MR] + z[MR:]
        return z[:, :BS] + z[:, BS:]

    def work(left_ref, list_ref, mirrored, into_ref, at, begin, end):
        def several(i, _):
            items = [item_ref[at, UNROLL * i + e] for e in range(UNROLL)]
            done = [product(left_ref, list_ref, mirrored, item >> 6, item & 63) for item in items]
            for item, z in zip(items, done):
                into_ref[item >> 6] += z.reshape(MR // 8, 8, BS)
            return 0

        lax.fori_loop(begin, end, several, 0)

    begin = 0
    for i, load in enumerate(loads):
        load.wait()
        end = limit_ref[4 + i]
        work(a_ref, st_ref, True, sum_ref, 1, begin, end)
        begin = end
    work(a_ref, sd_ref, False, sum_ref, 0, 0, limit_ref[0])

    def halves(k, _):
        high, low = split(sum_ref[k].reshape(MR, BS))
        s_ref[k, :MR] = high
        s_ref[k, MR:] = low
        return 0

    lax.fori_loop(0, NB, halves, 0, unroll=2)
    work(s_ref, pd_ref, False, cube_ref, 2, 0, limit_ref[2])
    work(s_ref, pt_ref, True, cube_ref, 3, 0, limit_ref[3])
    for j in range(COLS):
        out_ref[:, j * BS:(j + 1) * BS] = (3.0 * sum_ref[first_col + j] - 2.0 * cube_ref[j]).reshape(MR, BS)


def compact(chosen, codes, pad):
    ids = jnp.arange(NB, dtype=jnp.int32)
    at = jnp.where(chosen, prefix(chosen), -1)
    hit = at[:, :, None] == ids[None, None, :]
    table = pad + jnp.sum(jnp.where(hit, (codes - pad)[:, :, None], 0), axis=1)
    return jnp.pad(table, ((0, 1), (0, 0)), constant_values=pad)


def count(chosen):
    return jnp.sum(chosen.astype(jnp.int32), axis=1)


def flat_items(chosen, mirrored_table):
    columns = jnp.array([[x.shape[0]] for x in chosen], jnp.int32)
    pairs = jnp.stack([jnp.pad((count(x) + 1) >> 1, (0, NB - x.shape[0])) for x in chosen])
    begin = prefix(pairs)
    end = begin + pairs
    total = end[:, NB - 1:]
    p = jnp.arange(ITEMS, dtype=jnp.int32)
    before = end[:, None, :] <= p[None, :, None]
    column = jnp.sum(before.astype(jnp.int32), axis=2)
    offset = p[None, :] - jnp.max(jnp.where(before, end[:, None, :], 0), axis=2)
    items = jnp.where(p[None, :] < total, column * NB + 2 * offset, columns * NB)
    place = jnp.max(mirrored_table[:NB].reshape(NB, NB // 2, 2), axis=2) >> 10
    i = jnp.arange(NB // 2, dtype=jnp.int32)[None, :]
    at = jnp.where(i < pairs[1][:, None], begin[1][:, None] + i, ITEMS)
    ends = [
        jnp.minimum(jnp.min(jnp.where(place >= c * PART, at, ITEMS)), total[1, 0]) // UNROLL for c in range(1, PARTS)
    ]
    rounds = (total[:, 0] + UNROLL - 1) // UNROLL
    return items, jnp.concatenate([rounds, jnp.stack(ends), rounds[1:2]])


SMEM = pl.BlockSpec(memory_space=pltpu.SMEM)
INVMEM = pl.BlockSpec(memory_space=pltpu.VMEM)
ANY = pl.BlockSpec(memory_space=pl.ANY)


def gather(upper, pattern, first, last):
    ids = jnp.arange(NB, dtype=jnp.int32)
    row, col, depth = lax.axis_index("row"), lax.axis_index("col"), lax.axis_index("depth")
    packed = pl.pallas_call(
        pack_kernel,
        out_shape=jax.ShapeDtypeStruct((STRIPS, NCOL, SRC, 8, BS), jnp.float32),
        in_specs=[SMEM, SMEM, INVMEM, ANY],
        out_specs=INVMEM,
        scratch_shapes=[pltpu.SMEM((8 * SRC,), jnp.int32), pltpu.SemaphoreType.DMA((8 * SRC,))],
        compiler_params=pltpu.CompilerParams(vmem_limit_bytes=16 * 1024 * 1024),
    )(jnp.stack([row, col, depth]).astype(jnp.int32), pattern, pattern, upper.reshape(ROWS * STRIPS, 8, COLS * BS))
    got = lax.all_to_all(packed.reshape(NB, SRC * 8, BS), ("row", "col"), 0, 0, tiled=True)
    g = 8 * jnp.arange(PER, dtype=jnp.int32) + 2 * col + depth
    source = jnp.minimum(jnp.sum((last[None, :] <= g[:, None]).astype(jnp.int32), axis=1), NB - 1)
    source_first = jnp.sum(jnp.where(source[:, None] == ids[None, :], first[None, :], 0), axis=1)
    pick = source * SRC + jnp.clip((g - source_first) >> 3, 0, SRC - 1)
    share = pl.pallas_call(
        select_kernel,
        out_shape=jax.ShapeDtypeStruct((PER, 8, BS), jnp.float32),
        in_specs=[SMEM, INVMEM],
        out_specs=INVMEM,
        compiler_params=pltpu.CompilerParams(vmem_limit_bytes=16 * 1024 * 1024),
    )(pick, got.reshape(NB * SRC, 8, BS))
    return lax.all_gather(share, ALL, axis=0).reshape(STRIPS, 8, PER, 8, BS)


def work_lists(stored, slot):
    ids = jnp.arange(NB, dtype=jnp.int32)
    row, col, depth = lax.axis_index("row"), lax.axis_index("col"), lax.axis_index("depth")
    below = ids[:, None] > ids[None, :]
    both = jnp.where(below, stored.T, stored) != 0
    slots = jnp.where(below, slot.T, slot)
    codes = ids[None, :] + BS * slots
    my_row = row * ROWS + depth * HALF
    near = jnp.any(lax.dynamic_slice_in_dim(both, my_row, HALF, 0), axis=0)
    direct = both & (ids[None, :] <= ids[:, None])
    mirrored = both & (ids[None, :] > ids[:, None])
    sd, st = direct & near[None, :], mirrored & near[None, :]
    col_direct = lax.dynamic_slice_in_dim(direct, col * COLS, COLS, 0)
    col_mirrored = lax.dynamic_slice_in_dim(mirrored, col * COLS, COLS, 0)
    col_codes = lax.dynamic_slice_in_dim(codes, col * COLS, COLS, 0)
    row_both = lax.dynamic_slice_in_dim(both, my_row, HALF, 0)
    row_codes = lax.dynamic_slice_in_dim(codes + 65536 * below, my_row, HALF, 0)
    st_table = compact(st, codes, NB)
    items, limits = flat_items((sd, st, col_direct, col_mirrored), st_table)
    return (
        compact(sd, codes, NB), st_table, compact(col_direct, col_codes, NB), compact(col_mirrored, col_codes, NB),
        items, limits, compact(row_both, row_codes, NB), count(row_both), (col * COLS)[None].astype(jnp.int32),
    )


def multiply(upper, pattern, blocks, *lists):
    return pl.pallas_call(
        main_kernel,
        out_shape=jax.ShapeDtypeStruct((MR, COLS * BS), jnp.float32),
        in_specs=[SMEM] * 9 + [ANY],
        out_specs=INVMEM,
        scratch_shapes=[
            pltpu.VMEM((STRIPS, 8, PER, 8, BS), jnp.float32),
            pltpu.VMEM((NB + 1, 2 * MR, BS), jnp.bfloat16),
            pltpu.VMEM((NB + 1, 2 * MR, BS), jnp.bfloat16),
            pltpu.VMEM((NB + 1, MR // 8, 8, BS), jnp.float32),
            pltpu.VMEM((COLS + 1, MR // 8, 8, BS), jnp.float32),
            pltpu.SemaphoreType.DMA((PARTS,)),
            pltpu.SemaphoreType.DMA((HALF * NB,)),
        ],
        compiler_params=pltpu.CompilerParams(vmem_limit_bytes=VMEM),
    )(*lists, blocks)


def join_kernel(depth_ref, mine_ref, other_ref, out_ref, held_ref, in_sem, out_sem):
    depth = depth_ref[0]
    rows = MR // 4
    loads, stores = [], []
    for i in range(8):
        part_ref, half = ((mine_ref, depth), (other_ref, 1 - depth))[i % 2]
        at = i // 2 * rows
        to = pl.multiple_of(half * MR + at, rows)
        loads.append(pltpu.make_async_copy(part_ref.at[pl.ds(at, rows)], held_ref.at[i], in_sem.at[i]))
        stores.append(pltpu.make_async_copy(held_ref.at[i], out_ref.at[pl.ds(to, rows)], out_sem.at[i]))
    for load in loads:
        load.start()
    for load, store in zip(loads, stores):
        load.wait()
        store.start()
    for store in stores:
        store.wait()


def dense(upper, pattern):
    rows_tile, cols_tile = upper.shape
    nrow = lax.axis_size("row")
    ncol = lax.axis_size("col")
    ndep = lax.axis_size("depth")
    row_blocks = rows_tile // BS
    col_blocks = cols_tile // BS
    spread = upper.reshape(row_blocks, ncol, BS // ncol, col_blocks, nrow, BS // nrow)
    spread = spread.transpose(4, 1, 0, 2, 3, 5).reshape(
        nrow * ncol, row_blocks, BS // ncol, col_blocks, BS // nrow
    )
    spread = lax.all_to_all(spread, ("row", "col"), split_axis=0, concat_axis=0, tiled=True)
    spread = spread.reshape(nrow, ncol, row_blocks, BS // ncol, col_blocks, BS // nrow)
    spread = spread.transpose(0, 2, 3, 1, 4, 5).reshape(
        ncol, col_blocks, BS // ncol, nrow, row_blocks, BS // nrow
    )
    spread = spread.transpose(3, 0, 4, 5, 1, 2).reshape(
        nrow * ncol, row_blocks, BS // nrow, col_blocks, BS // ncol
    )
    spread = lax.all_to_all(spread, ("row", "col"), split_axis=0, concat_axis=0, tiled=True)
    spread = spread.reshape(nrow, ncol, row_blocks, BS // nrow, col_blocks, BS // ncol)
    mirror = spread.transpose(2, 0, 3, 4, 1, 5).reshape(row_blocks, BS, col_blocks, BS)
    row_index = lax.axis_index("row")
    col_index = lax.axis_index("col")
    row_first = row_index * row_blocks
    col_first = col_index * col_blocks
    global_rows = row_first + jnp.arange(row_blocks, dtype=jnp.int32)
    global_cols = col_first + jnp.arange(col_blocks, dtype=jnp.int32)
    above = global_rows[:, None] < global_cols[None, :]
    below = global_rows[:, None] > global_cols[None, :]
    upper_pat = lax.dynamic_slice(pattern, (row_first, col_first), (row_blocks, col_blocks))
    lower_pat = lax.dynamic_slice(pattern, (col_first, row_first), (col_blocks, row_blocks)).T
    keep = jnp.where(above, upper_pat, jnp.where(below, lower_pat, 1)).astype(jnp.float32)
    own = upper.reshape(row_blocks, BS, col_blocks, BS)
    blended = jnp.where(
        above[:, None, :, None],
        own,
        jnp.where(below[:, None, :, None], mirror, 0.5 * (own + mirror)),
    )
    density = (blended * keep[:, None, :, None]).reshape(rows_tile, cols_tile)
    layer = lax.axis_index("depth")

    def layer_columns(tile):
        split = tile.reshape(rows_tile, col_blocks // ndep, ndep, BS)
        return lax.dynamic_slice_in_dim(split, layer, 1, 2).reshape(
            rows_tile, col_blocks // ndep * BS
        )

    split_rows = density.reshape(row_blocks // ndep, ndep, BS, cols_tile)
    layer_rows = lax.dynamic_slice_in_dim(split_rows, layer, 1, 1).reshape(
        row_blocks // ndep * BS, cols_tile
    )
    panel = lax.all_gather(layer_rows, "row", axis=0, tiled=True)

    def accumulate(piece):
        return jnp.dot(
            piece, panel, precision=lax.Precision.HIGHEST, preferred_element_type=jnp.float32
        )

    square_part = accumulate(lax.all_gather(layer_columns(density), "col", axis=1, tiled=True))
    square = lax.psum(square_part, "depth")
    cube_part = accumulate(lax.all_gather(layer_columns(square), "col", axis=1, tiled=True))
    cube = lax.psum(cube_part, "depth")
    return 3.0 * square - 2.0 * cube


def dense_half(upper, pattern, *rest):
    return lax.dynamic_slice_in_dim(dense(upper, pattern), lax.axis_index("depth") * MR, MR, 0)


def local(upper, pattern):
    stored, slot, first, last, fits = layout(pattern)
    blocks = gather(upper, pattern, first, last)
    lists = lax.optimization_barrier(work_lists(stored, slot))
    mine = lax.cond(fits, multiply, dense_half, upper, pattern, blocks, *lists)
    other = lax.ppermute(mine, "depth", [(0, 1), (1, 0)])
    return pl.pallas_call(
        join_kernel,
        out_shape=jax.ShapeDtypeStruct(upper.shape, jnp.float32),
        in_specs=[SMEM, ANY, ANY],
        out_specs=ANY,
        scratch_shapes=[
            pltpu.VMEM((8, MR // 4, COLS * BS), jnp.float32),
            pltpu.SemaphoreType.DMA((8,)),
            pltpu.SemaphoreType.DMA((8,)),
        ],
        compiler_params=pltpu.CompilerParams(vmem_limit_bytes=16 * 1024 * 1024),
    )(lax.axis_index("depth")[None].astype(jnp.int32), mine, other)


def solution(mesh):
    placed = (P("row", "col"), P())
    return jax.shard_map(
        local, mesh=mesh, in_specs=placed, out_specs=P("row", "col"), check_vma=False
    )
```

```python
import jax
import jax.numpy as jnp
from jax import lax
from jax.experimental import pallas as pl
from jax.experimental.pallas import tpu as pltpu
from jax.sharding import PartitionSpec as P

BS = 128
NB = 64
ROWS = 4
COLS = 16
NROW = 16
NCOL = 4
STRIPS = 16
PER = 44
PARTS = 4
PART = PER // PARTS
ITEMS = 256
CAP = 8 * PER
SRC = 3
HALF = 2
MR = HALF * BS
UNROLL = 12
VMEM = 62 * 1024 * 1024
ALL = ("row", "col", "depth")


def prefix(ones):
    ids = jnp.arange(NB, dtype=jnp.int32)
    before = (ids[:, None] < ids[None, :]).astype(jnp.float32)
    return jnp.dot(ones.astype(jnp.float32), before, preferred_element_type=jnp.float32).astype(jnp.int32)


def layout(pattern):
    ids = jnp.arange(NB, dtype=jnp.int32)
    stored = jnp.where(ids[:, None] < ids[None, :], pattern, 0) + (ids[:, None] == ids[None, :])
    stored = (stored != 0).astype(jnp.int32)
    local = stored.reshape(NROW, ROWS, NCOL, COLS).transpose(0, 2, 1, 3).reshape(NB, NB)
    rank = prefix(local)
    count = jnp.sum(local, axis=1)
    first = prefix(count[None, :])[0]
    last = first + count
    slot = (first[:, None] + rank).reshape(NROW, NCOL, ROWS, COLS).transpose(0, 2, 1, 3).reshape(NB, NB)
    fits = jnp.all(count <= 8 * SRC) & (last[NB - 1] <= CAP)
    return stored, slot, first, last, fits


def pack_kernel(here_ref, pattern_ref, pattern_vec, upper_ref, out_ref, list_ref, sem):
    row, col, depth = here_ref[0], here_ref[1], here_ref[2]
    i = lax.broadcasted_iota(jnp.int32, (NB, NB), 0)
    j = lax.broadcasted_iota(jnp.int32, (NB, NB), 1)
    stored = (i == j) | ((i < j) & (pattern_vec[...] != 0))
    earlier = (i // ROWS) * NCOL + j // COLS < row * NCOL + col
    first = jnp.sum(jnp.where(stored & earlier, 1.0, 0.0)).astype(jnp.int32)

    def copy(at):
        code = list_ref[at]
        a, b, n = code & 3, (code >> 2) & 15, code >> 6
        return pltpu.make_async_copy(
            upper_ref.at[pl.ds(a * STRIPS, STRIPS), :, pl.ds(pl.multiple_of(b * BS, BS), BS)],
            out_ref.at[:, ((first + n) >> 1) & 3, n >> 3],
            sem.at[at],
        )

    def find(a, state):
        def one(b, state):
            n, at = state
            i, j = row * ROWS + a, col * COLS + b
            there = (i == j) | ((i < j) & (pattern_ref[i, j] != 0))
            ours = there & (((first + n) & 1) == depth) & (n < 8 * SRC)

            @pl.when(ours)
            def _():
                list_ref[at] = a + 4 * b + 64 * n
                copy(at).start()

            return n + there.astype(jnp.int32), at + ours.astype(jnp.int32)

        return lax.fori_loop(0, COLS, one, state, unroll=4)

    _, found = lax.fori_loop(0, ROWS, find, (jnp.int32(0), jnp.int32(0)))

    def finish(at, _):
        copy(at).wait()
        code = list_ref[at]
        a, b, n = code & 3, (code >> 2) & 15, code >> 6

        @pl.when(row * ROWS + a == col * COLS + b)
        def _():
            z = ((first + n) >> 1) & 3
            x = out_ref[:, z, n >> 3].reshape(BS, BS)
            out_ref[:, z, n >> 3] = (0.5 * (x + x.T)).reshape(STRIPS, 8, BS)

        return 0

    lax.fori_loop(0, found, finish, 0)


def select_kernel(index_ref, got_ref, out_ref):
    for u in range(PER):
        out_ref[u] = got_ref[index_ref[u]]


def split(x):
    high = x.astype(jnp.bfloat16)
    return high, (x - high.astype(jnp.float32)).astype(jnp.bfloat16)


def main_kernel(sd_ref, st_ref, pd_ref, pt_ref, item_ref, limit_ref, row_ref, rn_ref, where_ref,
                blocks_hbm, whole_hbm, half_hbm, out_ref, blocks_ref, a_ref, s_ref, sum_ref, cube_ref, sem, row_sem, out_sem):
    first_col = where_ref[0]
    first_row = pl.multiple_of(where_ref[1] * MR, MR)

    def row_load(h, p, n):
        slot = (row_ref[h, p] >> 7) & 511
        return pltpu.make_async_copy(
            blocks_hbm.at[:, slot & 7, slot >> 3], sum_ref.at[n >> 1, pl.ds((n & 1) * STRIPS, STRIPS)], row_sem.at[n]
        )

    for h in range(HALF):
        def start(p, _, h=h):
            row_load(h, p, h * NB + p).start()
            return 0

        lax.fori_loop(0, rn_ref[h], start, 0)
    loads = [
        pltpu.make_async_copy(
            blocks_hbm.at[:, :, pl.ds(i * PART, PART)], blocks_ref.at[:, :, pl.ds(i * PART, PART)], sem.at[i]
        )
        for i in range(PARTS)
    ]
    for load in loads:
        load.start()
    a_ref[...] = jnp.zeros_like(a_ref)
    cube_ref[...] = jnp.zeros_like(cube_ref)
    s_ref[NB] = jnp.zeros((2 * MR, BS), jnp.bfloat16)

    def block(slot):
        return blocks_ref[:, slot & 7, slot >> 3].reshape(BS, BS)

    for h in range(HALF):
        def fill(p, _, h=h):
            code = row_ref[h, p]
            m = code & 127
            n = h * NB + p
            row_load(h, p, n).wait()
            x = sum_ref[n >> 1, pl.ds((n & 1) * STRIPS, STRIPS)].reshape(BS, BS)

            def put(x):
                high, low = split(x)
                a_ref[m, h * BS:(h + 1) * BS] = high
                a_ref[m, MR + h * BS:MR + (h + 1) * BS] = low

            @pl.when(code < 65536)
            def _():
                put(x)

            @pl.when(code >= 65536)
            def _():
                put(x.T)

            return 0

        lax.fori_loop(0, rn_ref[h], fill, 0)
    sum_ref[...] = jnp.zeros_like(sum_ref)

    def product(left_ref, list_ref, mirrored, k, p):
        c0, c1 = list_ref[k, p], list_ref[k, p + 1]
        left = jnp.concatenate([left_ref[c0 & 127], left_ref[c1 & 127]], axis=1)
        h0, l0 = split(block(c0 >> 7))
        h1, l1 = split(block(c1 >> 7))
        if mirrored:
            right = jnp.concatenate([jnp.concatenate([h0, h1], axis=1), jnp.concatenate([l0, l1], axis=1)], axis=0)
            z = lax.dot_general(left, right, (((1,), (1,)), ((), ())), preferred_element_type=jnp.float32)
        else:
            right = jnp.concatenate([jnp.concatenate([h0, l0], axis=1), jnp.concatenate([h1, l1], axis=1)], axis=0)
            z = jnp.dot(left, right, preferred_element_type=jnp.float32)
        z = z[:MR] + z[MR:]
        return z[:, :BS] + z[:, BS:]

    def work(left_ref, list_ref, mirrored, into_ref, at, begin, end):
        def several(i, _):
            items = [item_ref[at, UNROLL * i + e] for e in range(UNROLL)]
            done = [product(left_ref, list_ref, mirrored, item >> 6, item & 63) for item in items]
            for item, z in zip(items, done):
                into_ref[item >> 6] += z.reshape(MR // 8, 8, BS)
            return 0

        lax.fori_loop(begin, end, several, 0)

    begin = 0
    for i, load in enumerate(loads):
        load.wait()
        end = limit_ref[4 + i]
        work(a_ref, st_ref, True, sum_ref, 1, begin, end)
        begin = end
    work(a_ref, sd_ref, False, sum_ref, 0, 0, limit_ref[0])

    def halves(k, _):
        high, low = split(sum_ref[k].reshape(MR, BS))
        s_ref[k, :MR] = high
        s_ref[k, MR:] = low
        return 0

    lax.fori_loop(0, NB, halves, 0, unroll=2)
    work(s_ref, pd_ref, False, cube_ref, 2, 0, limit_ref[2])
    work(s_ref, pt_ref, True, cube_ref, 3, 0, limit_ref[3])
    stores = []
    for j in range(COLS):
        out_ref[:, j * BS:(j + 1) * BS] = (3.0 * sum_ref[first_col + j] - 2.0 * cube_ref[j]).reshape(MR, BS)
        if j % 4 == 3:
            columns = pl.ds((j - 3) * BS, 4 * BS)
            for k, to in enumerate((half_hbm.at[:, columns], whole_hbm.at[pl.ds(first_row, MR), columns])):
                stores.append(pltpu.make_async_copy(out_ref.at[:, columns], to, out_sem.at[k, j // 4]))
                stores[-1].start()
    for store in stores:
        store.wait()


def compact(chosen, codes, pad):
    ids = jnp.arange(NB, dtype=jnp.int32)
    at = jnp.where(chosen, prefix(chosen), -1)
    hit = at[:, :, None] == ids[None, None, :]
    table = pad + jnp.sum(jnp.where(hit, (codes - pad)[:, :, None], 0), axis=1)
    return jnp.pad(table, ((0, 1), (0, 0)), constant_values=pad)


def count(chosen):
    return jnp.sum(chosen.astype(jnp.int32), axis=1)


def flat_items(chosen, mirrored_table):
    columns = jnp.array([[x.shape[0]] for x in chosen], jnp.int32)
    pairs = jnp.stack([jnp.pad((count(x) + 1) >> 1, (0, NB - x.shape[0])) for x in chosen])
    begin = prefix(pairs)
    end = begin + pairs
    total = end[:, NB - 1:]
    p = jnp.arange(ITEMS, dtype=jnp.int32)
    before = end[:, None, :] <= p[None, :, None]
    column = jnp.sum(before.astype(jnp.int32), axis=2)
    offset = p[None, :] - jnp.max(jnp.where(before, end[:, None, :], 0), axis=2)
    items = jnp.where(p[None, :] < total, column * NB + 2 * offset, columns * NB)
    place = jnp.max(mirrored_table[:NB].reshape(NB, NB // 2, 2), axis=2) >> 10
    i = jnp.arange(NB // 2, dtype=jnp.int32)[None, :]
    at = jnp.where(i < pairs[1][:, None], begin[1][:, None] + i, ITEMS)
    ends = [
        jnp.minimum(jnp.min(jnp.where(place >= c * PART, at, ITEMS)), total[1, 0]) // UNROLL for c in range(1, PARTS)
    ]
    rounds = (total[:, 0] + UNROLL - 1) // UNROLL
    return items, jnp.concatenate([rounds, jnp.stack(ends), rounds[1:2]])


SMEM = pl.BlockSpec(memory_space=pltpu.SMEM)
INVMEM = pl.BlockSpec(memory_space=pltpu.VMEM)
ANY = pl.BlockSpec(memory_space=pl.ANY)


def gather(upper, pattern, first, last):
    ids = jnp.arange(NB, dtype=jnp.int32)
    row, col, depth = lax.axis_index("row"), lax.axis_index("col"), lax.axis_index("depth")
    packed = pl.pallas_call(
        pack_kernel,
        out_shape=jax.ShapeDtypeStruct((STRIPS, NCOL, SRC, 8, BS), jnp.float32),
        in_specs=[SMEM, SMEM, INVMEM, ANY],
        out_specs=INVMEM,
        scratch_shapes=[pltpu.SMEM((8 * SRC,), jnp.int32), pltpu.SemaphoreType.DMA((8 * SRC,))],
        compiler_params=pltpu.CompilerParams(vmem_limit_bytes=16 * 1024 * 1024),
    )(jnp.stack([row, col, depth]).astype(jnp.int32), pattern, pattern, upper.reshape(ROWS * STRIPS, 8, COLS * BS))
    got = lax.all_to_all(packed.reshape(NB, SRC * 8, BS), ("row", "col"), 0, 0, tiled=True)
    g = 8 * jnp.arange(PER, dtype=jnp.int32) + 2 * col + depth
    source = jnp.minimum(jnp.sum((last[None, :] <= g[:, None]).astype(jnp.int32), axis=1), NB - 1)
    source_first = jnp.sum(jnp.where(source[:, None] == ids[None, :], first[None, :], 0), axis=1)
    pick = source * SRC + jnp.clip((g - source_first) >> 3, 0, SRC - 1)
    share = pl.pallas_call(
        select_kernel,
        out_shape=jax.ShapeDtypeStruct((PER, 8, BS), jnp.float32),
        in_specs=[SMEM, INVMEM],
        out_specs=INVMEM,
        compiler_params=pltpu.CompilerParams(vmem_limit_bytes=16 * 1024 * 1024),
    )(pick, got.reshape(NB * SRC, 8, BS))
    return lax.all_gather(share, ALL, axis=0).reshape(STRIPS, 8, PER, 8, BS)


def work_lists(stored, slot):
    ids = jnp.arange(NB, dtype=jnp.int32)
    row, col, depth = lax.axis_index("row"), lax.axis_index("col"), lax.axis_index("depth")
    below = ids[:, None] > ids[None, :]
    both = jnp.where(below, stored.T, stored) != 0
    slots = jnp.where(below, slot.T, slot)
    codes = ids[None, :] + BS * slots
    my_row = row * ROWS + depth * HALF
    near = jnp.any(lax.dynamic_slice_in_dim(both, my_row, HALF, 0), axis=0)
    direct = both & (ids[None, :] <= ids[:, None])
    mirrored = both & (ids[None, :] > ids[:, None])
    sd, st = direct & near[None, :], mirrored & near[None, :]
    col_direct = lax.dynamic_slice_in_dim(direct, col * COLS, COLS, 0)
    col_mirrored = lax.dynamic_slice_in_dim(mirrored, col * COLS, COLS, 0)
    col_codes = lax.dynamic_slice_in_dim(codes, col * COLS, COLS, 0)
    row_both = lax.dynamic_slice_in_dim(both, my_row, HALF, 0)
    row_codes = lax.dynamic_slice_in_dim(codes + 65536 * below, my_row, HALF, 0)
    st_table = compact(st, codes, NB)
    items, limits = flat_items((sd, st, col_direct, col_mirrored), st_table)
    return (
        compact(sd, codes, NB), st_table, compact(col_direct, col_codes, NB), compact(col_mirrored, col_codes, NB),
        items, limits, compact(row_both, row_codes, NB), count(row_both), jnp.stack([col * COLS, depth]).astype(jnp.int32),
    )


def multiply(upper, pattern, blocks, *lists):
    whole, half = pl.pallas_call(
        main_kernel,
        out_shape=[
            jax.ShapeDtypeStruct((2 * MR, COLS * BS), jnp.float32),
            jax.ShapeDtypeStruct((MR, COLS * BS), jnp.float32),
        ],
        in_specs=[SMEM] * 9 + [ANY],
        out_specs=[ANY, ANY],
        scratch_shapes=[
            pltpu.VMEM((MR, COLS * BS), jnp.float32),
            pltpu.VMEM((STRIPS, 8, PER, 8, BS), jnp.float32),
            pltpu.VMEM((NB + 1, 2 * MR, BS), jnp.bfloat16),
            pltpu.VMEM((NB + 1, 2 * MR, BS), jnp.bfloat16),
            pltpu.VMEM((NB + 1, MR // 8, 8, BS), jnp.float32),
            pltpu.VMEM((COLS + 1, MR // 8, 8, BS), jnp.float32),
            pltpu.SemaphoreType.DMA((PARTS,)),
            pltpu.SemaphoreType.DMA((HALF * NB,)),
            pltpu.SemaphoreType.DMA((2, 4)),
        ],
        compiler_params=pltpu.CompilerParams(vmem_limit_bytes=VMEM),
    )(*lists, blocks)
    return whole, half


def join_kernel(depth_ref, whole_ref, other_ref, out_ref, held_ref, in_sem, out_sem):
    first_row = (1 - depth_ref[0]) * MR
    rows = MR // 4
    loads, stores = [], []
    for i in range(4):
        to = pl.multiple_of(first_row + i * rows, rows)
        loads.append(pltpu.make_async_copy(other_ref.at[pl.ds(i * rows, rows)], held_ref.at[i], in_sem.at[i]))
        stores.append(pltpu.make_async_copy(held_ref.at[i], out_ref.at[pl.ds(to, rows)], out_sem.at[i]))
    for load in loads:
        load.start()
    for load, store in zip(loads, stores):
        load.wait()
        store.start()
    for store in stores:
        store.wait()


def dense(upper, pattern):
    rows_tile, cols_tile = upper.shape
    nrow = lax.axis_size("row")
    ncol = lax.axis_size("col")
    ndep = lax.axis_size("depth")
    row_blocks = rows_tile // BS
    col_blocks = cols_tile // BS
    spread = upper.reshape(row_blocks, ncol, BS // ncol, col_blocks, nrow, BS // nrow)
    spread = spread.transpose(4, 1, 0, 2, 3, 5).reshape(
        nrow * ncol, row_blocks, BS // ncol, col_blocks, BS // nrow
    )
    spread = lax.all_to_all(spread, ("row", "col"), split_axis=0, concat_axis=0, tiled=True)
    spread = spread.reshape(nrow, ncol, row_blocks, BS // ncol, col_blocks, BS // nrow)
    spread = spread.transpose(0, 2, 3, 1, 4, 5).reshape(
        ncol, col_blocks, BS // ncol, nrow, row_blocks, BS // nrow
    )
    spread = spread.transpose(3, 0, 4, 5, 1, 2).reshape(
        nrow * ncol, row_blocks, BS // nrow, col_blocks, BS // ncol
    )
    spread = lax.all_to_all(spread, ("row", "col"), split_axis=0, concat_axis=0, tiled=True)
    spread = spread.reshape(nrow, ncol, row_blocks, BS // nrow, col_blocks, BS // ncol)
    mirror = spread.transpose(2, 0, 3, 4, 1, 5).reshape(row_blocks, BS, col_blocks, BS)
    row_index = lax.axis_index("row")
    col_index = lax.axis_index("col")
    row_first = row_index * row_blocks
    col_first = col_index * col_blocks
    global_rows = row_first + jnp.arange(row_blocks, dtype=jnp.int32)
    global_cols = col_first + jnp.arange(col_blocks, dtype=jnp.int32)
    above = global_rows[:, None] < global_cols[None, :]
    below = global_rows[:, None] > global_cols[None, :]
    upper_pat = lax.dynamic_slice(pattern, (row_first, col_first), (row_blocks, col_blocks))
    lower_pat = lax.dynamic_slice(pattern, (col_first, row_first), (col_blocks, row_blocks)).T
    keep = jnp.where(above, upper_pat, jnp.where(below, lower_pat, 1)).astype(jnp.float32)
    own = upper.reshape(row_blocks, BS, col_blocks, BS)
    blended = jnp.where(
        above[:, None, :, None],
        own,
        jnp.where(below[:, None, :, None], mirror, 0.5 * (own + mirror)),
    )
    density = (blended * keep[:, None, :, None]).reshape(rows_tile, cols_tile)
    layer = lax.axis_index("depth")

    def layer_columns(tile):
        split = tile.reshape(rows_tile, col_blocks // ndep, ndep, BS)
        return lax.dynamic_slice_in_dim(split, layer, 1, 2).reshape(
            rows_tile, col_blocks // ndep * BS
        )

    split_rows = density.reshape(row_blocks // ndep, ndep, BS, cols_tile)
    layer_rows = lax.dynamic_slice_in_dim(split_rows, layer, 1, 1).reshape(
        row_blocks // ndep * BS, cols_tile
    )
    panel = lax.all_gather(layer_rows, "row", axis=0, tiled=True)

    def accumulate(piece):
        return jnp.dot(
            piece, panel, precision=lax.Precision.HIGHEST, preferred_element_type=jnp.float32
        )

    square_part = accumulate(lax.all_gather(layer_columns(density), "col", axis=1, tiled=True))
    square = lax.psum(square_part, "depth")
    cube_part = accumulate(lax.all_gather(layer_columns(square), "col", axis=1, tiled=True))
    cube = lax.psum(cube_part, "depth")
    return 3.0 * square - 2.0 * cube


def dense_halves(upper, pattern, *rest):
    whole = dense(upper, pattern)
    return whole, lax.dynamic_slice_in_dim(whole, lax.axis_index("depth") * MR, MR, 0)


def local(upper, pattern):
    stored, slot, first, last, fits = layout(pattern)
    blocks = gather(upper, pattern, first, last)
    lists = lax.optimization_barrier(work_lists(stored, slot))
    whole, mine = lax.cond(fits, multiply, dense_halves, upper, pattern, blocks, *lists)
    other = lax.ppermute(mine, "depth", [(0, 1), (1, 0)])
    return pl.pallas_call(
        join_kernel,
        out_shape=jax.ShapeDtypeStruct(upper.shape, jnp.float32),
        in_specs=[SMEM, ANY, ANY],
        out_specs=ANY,
        input_output_aliases={1: 0},
        scratch_shapes=[
            pltpu.VMEM((4, MR // 4, COLS * BS), jnp.float32),
            pltpu.SemaphoreType.DMA((4,)),
            pltpu.SemaphoreType.DMA((4,)),
        ],
        compiler_params=pltpu.CompilerParams(vmem_limit_bytes=16 * 1024 * 1024),
    )(lax.axis_index("depth")[None].astype(jnp.int32), whole, other)


def solution(mesh):
    placed = (P("row", "col"), P())
    return jax.shard_map(
        local, mesh=mesh, in_specs=placed, out_specs=P("row", "col"), check_vma=False
    )
```

```python
import jax
import jax.numpy as jnp
from jax import lax
from jax.experimental import pallas as pl
from jax.experimental.pallas import tpu as pltpu
from jax.sharding import PartitionSpec as P

BS = 128
NB = 64
ROWS = 4
COLS = 16
NROW = 16
NCOL = 4
STRIPS = 16
PER = 44
PARTS = 4
PART = PER // PARTS
ITEMS = 256
CAP = 8 * PER
SRC = 3
HALF = 2
MR = HALF * BS
UNROLL = 16
VMEM = 62 * 1024 * 1024
ALL = ("row", "col", "depth")


def prefix(ones):
    ids = jnp.arange(NB, dtype=jnp.int32)
    before = (ids[:, None] < ids[None, :]).astype(jnp.float32)
    return jnp.dot(ones.astype(jnp.float32), before, preferred_element_type=jnp.float32).astype(jnp.int32)


def layout(pattern):
    ids = jnp.arange(NB, dtype=jnp.int32)
    stored = jnp.where(ids[:, None] < ids[None, :], pattern, 0) + (ids[:, None] == ids[None, :])
    stored = (stored != 0).astype(jnp.int32)
    local = stored.reshape(NROW, ROWS, NCOL, COLS).transpose(0, 2, 1, 3).reshape(NB, NB)
    rank = prefix(local)
    count = jnp.sum(local, axis=1)
    first = prefix(count[None, :])[0]
    last = first + count
    slot = (first[:, None] + rank).reshape(NROW, NCOL, ROWS, COLS).transpose(0, 2, 1, 3).reshape(NB, NB)
    fits = jnp.all(count <= 8 * SRC) & (last[NB - 1] <= CAP)
    return stored, slot, first, last, fits


def pack_kernel(here_ref, pattern_ref, pattern_vec, upper_ref, out_ref, list_ref, sem):
    row, col, depth = here_ref[0], here_ref[1], here_ref[2]
    i = lax.broadcasted_iota(jnp.int32, (NB, NB), 0)
    j = lax.broadcasted_iota(jnp.int32, (NB, NB), 1)
    stored = (i == j) | ((i < j) & (pattern_vec[...] != 0))
    earlier = (i // ROWS) * NCOL + j // COLS < row * NCOL + col
    first = jnp.sum(jnp.where(stored & earlier, 1.0, 0.0)).astype(jnp.int32)

    def copy(at):
        code = list_ref[at]
        a, b, n = code & 3, (code >> 2) & 15, code >> 6
        return pltpu.make_async_copy(
            upper_ref.at[pl.ds(a * STRIPS, STRIPS), :, pl.ds(pl.multiple_of(b * BS, BS), BS)],
            out_ref.at[:, ((first + n) >> 1) & 3, n >> 3],
            sem.at[at],
        )

    def find(a, state):
        def one(b, state):
            n, at = state
            i, j = row * ROWS + a, col * COLS + b
            there = (i == j) | ((i < j) & (pattern_ref[i, j] != 0))
            ours = there & (((first + n) & 1) == depth) & (n < 8 * SRC)

            @pl.when(ours)
            def _():
                list_ref[at] = a + 4 * b + 64 * n
                copy(at).start()

            return n + there.astype(jnp.int32), at + ours.astype(jnp.int32)

        return lax.fori_loop(0, COLS, one, state, unroll=4)

    _, found = lax.fori_loop(0, ROWS, find, (jnp.int32(0), jnp.int32(0)))

    def finish(at, _):
        copy(at).wait()
        code = list_ref[at]
        a, b, n = code & 3, (code >> 2) & 15, code >> 6

        @pl.when(row * ROWS + a == col * COLS + b)
        def _():
            z = ((first + n) >> 1) & 3
            x = out_ref[:, z, n >> 3].reshape(BS, BS)
            out_ref[:, z, n >> 3] = (0.5 * (x + x.T)).reshape(STRIPS, 8, BS)

        return 0

    lax.fori_loop(0, found, finish, 0)


def select_kernel(index_ref, got_ref, out_ref):
    for u in range(PER):
        out_ref[u] = got_ref[index_ref[u]]


def split(x):
    high = x.astype(jnp.bfloat16)
    return high, (x - high.astype(jnp.float32)).astype(jnp.bfloat16)


def main_kernel(sd_ref, st_ref, pd_ref, pt_ref, item_ref, limit_ref, row_ref, rn_ref, where_ref,
                blocks_hbm, whole_hbm, half_hbm, out_ref, blocks_ref, a_ref, s_ref, sum_ref, cube_ref, sem, row_sem, out_sem):
    first_col = where_ref[0]
    first_row = pl.multiple_of(where_ref[1] * MR, MR)

    def row_load(h, p, n):
        slot = (row_ref[h, p] >> 7) & 511
        return pltpu.make_async_copy(
            blocks_hbm.at[:, slot & 7, slot >> 3], sum_ref.at[n >> 1, pl.ds((n & 1) * STRIPS, STRIPS)], row_sem.at[n]
        )

    for h in range(HALF):
        def start(p, _, h=h):
            row_load(h, p, h * NB + p).start()
            return 0

        lax.fori_loop(0, rn_ref[h], start, 0)
    loads = [
        pltpu.make_async_copy(
            blocks_hbm.at[:, :, pl.ds(i * PART, PART)], blocks_ref.at[:, :, pl.ds(i * PART, PART)], sem.at[i]
        )
        for i in range(PARTS)
    ]
    for load in loads:
        load.start()
    a_ref[...] = jnp.zeros_like(a_ref)

    def clear(i, _):
        sum_ref[i] = jnp.zeros((MR // 8, 8, BS), jnp.float32)
        return 0

    used = [(rn_ref[h] + 1) >> 1 for h in range(HALF)]
    for h in range(HALF):
        lax.fori_loop(h * NB // 2 + used[h], (h + 1) * NB // 2, clear, 0)
    clear(NB, 0)
    cube_ref[...] = jnp.zeros_like(cube_ref)
    s_ref[NB] = jnp.zeros((2 * MR, BS), jnp.bfloat16)

    def block(slot):
        return blocks_ref[:, slot & 7, slot >> 3].reshape(BS, BS)

    for h in range(HALF):
        def fill(p, _, h=h):
            code = row_ref[h, p]
            m = code & 127
            n = h * NB + p
            row_load(h, p, n).wait()
            x = sum_ref[n >> 1, pl.ds((n & 1) * STRIPS, STRIPS)].reshape(BS, BS)

            def put(x):
                high, low = split(x)
                a_ref[m, h * BS:(h + 1) * BS] = high
                a_ref[m, MR + h * BS:MR + (h + 1) * BS] = low

            @pl.when(code < 65536)
            def _():
                put(x)

            @pl.when(code >= 65536)
            def _():
                put(x.T)

            return 0

        lax.fori_loop(0, rn_ref[h], fill, 0)
    for h in range(HALF):
        lax.fori_loop(h * NB // 2, h * NB // 2 + used[h], clear, 0)

    def product(left_ref, list_ref, mirrored, k, p):
        c0, c1 = list_ref[k, p], list_ref[k, p + 1]
        left = jnp.concatenate([left_ref[c0 & 127], left_ref[c1 & 127]], axis=1)
        h0, l0 = split(block(c0 >> 7))
        h1, l1 = split(block(c1 >> 7))
        if mirrored:
            right = jnp.concatenate([jnp.concatenate([h0, h1], axis=1), jnp.concatenate([l0, l1], axis=1)], axis=0)
            z = lax.dot_general(left, right, (((1,), (1,)), ((), ())), preferred_element_type=jnp.float32)
        else:
            right = jnp.concatenate([jnp.concatenate([h0, l0], axis=1), jnp.concatenate([h1, l1], axis=1)], axis=0)
            z = jnp.dot(left, right, preferred_element_type=jnp.float32)
        z = z[:MR] + z[MR:]
        return z[:, :BS] + z[:, BS:]

    def work(left_ref, list_ref, mirrored, into_ref, at, begin, end):
        def several(i, _):
            items = [item_ref[at, UNROLL * i + e] for e in range(UNROLL)]
            done = [product(left_ref, list_ref, mirrored, item >> 6, item & 63) for item in items]
            for item, z in zip(items, done):
                into_ref[item >> 6] += z.reshape(MR // 8, 8, BS)
            return 0

        lax.fori_loop(begin, end, several, 0)

    begin = 0
    for i, load in enumerate(loads):
        load.wait()
        end = limit_ref[4 + i]
        work(a_ref, st_ref, True, sum_ref, 1, begin, end)
        begin = end
    work(a_ref, sd_ref, False, sum_ref, 0, 0, limit_ref[0])

    def halves(k, _):
        high, low = split(sum_ref[k].reshape(MR, BS))
        s_ref[k, :MR] = high
        s_ref[k, MR:] = low
        return 0

    lax.fori_loop(0, NB, halves, 0, unroll=2)
    work(s_ref, pd_ref, False, cube_ref, 2, 0, limit_ref[2])
    work(s_ref, pt_ref, True, cube_ref, 3, 0, limit_ref[3])
    stores = []
    for j in range(COLS):
        out_ref[:, j * BS:(j + 1) * BS] = (3.0 * sum_ref[first_col + j] - 2.0 * cube_ref[j]).reshape(MR, BS)
        if j % 4 == 3:
            columns = pl.ds((j - 3) * BS, 4 * BS)
            for k, to in enumerate((half_hbm.at[:, columns], whole_hbm.at[pl.ds(first_row, MR), columns])):
                stores.append(pltpu.make_async_copy(out_ref.at[:, columns], to, out_sem.at[k, j // 4]))
                stores[-1].start()
    for store in stores:
        store.wait()


def compact(chosen, codes, pad):
    ids = jnp.arange(NB, dtype=jnp.int32)
    at = jnp.where(chosen, prefix(chosen), -1)
    hit = at[:, :, None] == ids[None, None, :]
    table = pad + jnp.sum(jnp.where(hit, (codes - pad)[:, :, None], 0), axis=1)
    return jnp.pad(table, ((0, 1), (0, 0)), constant_values=pad)


def count(chosen):
    return jnp.sum(chosen.astype(jnp.int32), axis=1)


def flat_items(chosen, mirrored_table):
    columns = jnp.array([[x.shape[0]] for x in chosen], jnp.int32)
    pairs = jnp.stack([jnp.pad((count(x) + 1) >> 1, (0, NB - x.shape[0])) for x in chosen])
    begin = prefix(pairs)
    end = begin + pairs
    total = end[:, NB - 1:]
    p = jnp.arange(ITEMS, dtype=jnp.int32)
    before = end[:, None, :] <= p[None, :, None]
    column = jnp.sum(before.astype(jnp.int32), axis=2)
    offset = p[None, :] - jnp.max(jnp.where(before, end[:, None, :], 0), axis=2)
    items = jnp.where(p[None, :] < total, column * NB + 2 * offset, columns * NB)
    place = jnp.max(mirrored_table[:NB].reshape(NB, NB // 2, 2), axis=2) >> 10
    i = jnp.arange(NB // 2, dtype=jnp.int32)[None, :]
    at = jnp.where(i < pairs[1][:, None], begin[1][:, None] + i, ITEMS)
    ends = [
        jnp.minimum(jnp.min(jnp.where(place >= c * PART, at, ITEMS)), total[1, 0]) // UNROLL for c in range(1, PARTS)
    ]
    rounds = (total[:, 0] + UNROLL - 1) // UNROLL
    return items, jnp.concatenate([rounds, jnp.stack(ends), rounds[1:2]])


SMEM = pl.BlockSpec(memory_space=pltpu.SMEM)
INVMEM = pl.BlockSpec(memory_space=pltpu.VMEM)
ANY = pl.BlockSpec(memory_space=pl.ANY)


def gather(upper, pattern, first, last):
    ids = jnp.arange(NB, dtype=jnp.int32)
    row, col, depth = lax.axis_index("row"), lax.axis_index("col"), lax.axis_index("depth")
    packed = pl.pallas_call(
        pack_kernel,
        out_shape=jax.ShapeDtypeStruct((STRIPS, NCOL, SRC, 8, BS), jnp.float32),
        in_specs=[SMEM, SMEM, INVMEM, ANY],
        out_specs=INVMEM,
        scratch_shapes=[pltpu.SMEM((8 * SRC,), jnp.int32), pltpu.SemaphoreType.DMA((8 * SRC,))],
        compiler_params=pltpu.CompilerParams(vmem_limit_bytes=16 * 1024 * 1024),
    )(jnp.stack([row, col, depth]).astype(jnp.int32), pattern, pattern, upper.reshape(ROWS * STRIPS, 8, COLS * BS))
    got = lax.all_to_all(packed.reshape(NB, SRC * 8, BS), ("row", "col"), 0, 0, tiled=True)
    g = 8 * jnp.arange(PER, dtype=jnp.int32) + 2 * col + depth
    source = jnp.minimum(jnp.sum((last[None, :] <= g[:, None]).astype(jnp.int32), axis=1), NB - 1)
    source_first = jnp.sum(jnp.where(source[:, None] == ids[None, :], first[None, :], 0), axis=1)
    pick = source * SRC + jnp.clip((g - source_first) >> 3, 0, SRC - 1)
    share = pl.pallas_call(
        select_kernel,
        out_shape=jax.ShapeDtypeStruct((PER, 8, BS), jnp.float32),
        in_specs=[SMEM, INVMEM],
        out_specs=INVMEM,
        compiler_params=pltpu.CompilerParams(vmem_limit_bytes=16 * 1024 * 1024),
    )(pick, got.reshape(NB * SRC, 8, BS))
    return lax.all_gather(share, ALL, axis=0).reshape(STRIPS, 8, PER, 8, BS)


def work_lists(stored, slot):
    ids = jnp.arange(NB, dtype=jnp.int32)
    row, col, depth = lax.axis_index("row"), lax.axis_index("col"), lax.axis_index("depth")
    below = ids[:, None] > ids[None, :]
    both = jnp.where(below, stored.T, stored) != 0
    slots = jnp.where(below, slot.T, slot)
    codes = ids[None, :] + BS * slots
    my_row = row * ROWS + depth * HALF
    near = jnp.any(lax.dynamic_slice_in_dim(both, my_row, HALF, 0), axis=0)
    direct = both & (ids[None, :] <= ids[:, None])
    mirrored = both & (ids[None, :] > ids[:, None])
    sd, st = direct & near[None, :], mirrored & near[None, :]
    col_direct = lax.dynamic_slice_in_dim(direct, col * COLS, COLS, 0)
    col_mirrored = lax.dynamic_slice_in_dim(mirrored, col * COLS, COLS, 0)
    col_codes = lax.dynamic_slice_in_dim(codes, col * COLS, COLS, 0)
    row_both = lax.dynamic_slice_in_dim(both, my_row, HALF, 0)
    row_codes = lax.dynamic_slice_in_dim(codes + 65536 * below, my_row, HALF, 0)
    st_table = compact(st, codes, NB)
    items, limits = flat_items((sd, st, col_direct, col_mirrored), st_table)
    return (
        compact(sd, codes, NB), st_table, compact(col_direct, col_codes, NB), compact(col_mirrored, col_codes, NB),
        items, limits, compact(row_both, row_codes, NB), count(row_both), jnp.stack([col * COLS, depth]).astype(jnp.int32),
    )


def multiply(upper, pattern, blocks, *lists):
    whole, half = pl.pallas_call(
        main_kernel,
        out_shape=[
            jax.ShapeDtypeStruct((2 * MR, COLS * BS), jnp.float32),
            jax.ShapeDtypeStruct((MR, COLS * BS), jnp.float32),
        ],
        in_specs=[SMEM] * 9 + [ANY],
        out_specs=[ANY, ANY],
        scratch_shapes=[
            pltpu.VMEM((MR, COLS * BS), jnp.float32),
            pltpu.VMEM((STRIPS, 8, PER, 8, BS), jnp.float32),
            pltpu.VMEM((NB + 1, 2 * MR, BS), jnp.bfloat16),
            pltpu.VMEM((NB + 1, 2 * MR, BS), jnp.bfloat16),
            pltpu.VMEM((NB + 1, MR // 8, 8, BS), jnp.float32),
            pltpu.VMEM((COLS + 1, MR // 8, 8, BS), jnp.float32),
            pltpu.SemaphoreType.DMA((PARTS,)),
            pltpu.SemaphoreType.DMA((HALF * NB,)),
            pltpu.SemaphoreType.DMA((2, 4)),
        ],
        compiler_params=pltpu.CompilerParams(vmem_limit_bytes=VMEM),
    )(*lists, blocks)
    return whole, half


def join_kernel(depth_ref, whole_ref, other_ref, out_ref, held_ref, in_sem, out_sem):
    first_row = (1 - depth_ref[0]) * MR
    rows = MR // 4
    loads, stores = [], []
    for i in range(4):
        to = pl.multiple_of(first_row + i * rows, rows)
        loads.append(pltpu.make_async_copy(other_ref.at[pl.ds(i * rows, rows)], held_ref.at[i], in_sem.at[i]))
        stores.append(pltpu.make_async_copy(held_ref.at[i], out_ref.at[pl.ds(to, rows)], out_sem.at[i]))
    for load in loads:
        load.start()
    for load, store in zip(loads, stores):
        load.wait()
        store.start()
    for store in stores:
        store.wait()


def dense(upper, pattern):
    rows_tile, cols_tile = upper.shape
    nrow = lax.axis_size("row")
    ncol = lax.axis_size("col")
    ndep = lax.axis_size("depth")
    row_blocks = rows_tile // BS
    col_blocks = cols_tile // BS
    spread = upper.reshape(row_blocks, ncol, BS // ncol, col_blocks, nrow, BS // nrow)
    spread = spread.transpose(4, 1, 0, 2, 3, 5).reshape(
        nrow * ncol, row_blocks, BS // ncol, col_blocks, BS // nrow
    )
    spread = lax.all_to_all(spread, ("row", "col"), split_axis=0, concat_axis=0, tiled=True)
    spread = spread.reshape(nrow, ncol, row_blocks, BS // ncol, col_blocks, BS // nrow)
    spread = spread.transpose(0, 2, 3, 1, 4, 5).reshape(
        ncol, col_blocks, BS // ncol, nrow, row_blocks, BS // nrow
    )
    spread = spread.transpose(3, 0, 4, 5, 1, 2).reshape(
        nrow * ncol, row_blocks, BS // nrow, col_blocks, BS // ncol
    )
    spread = lax.all_to_all(spread, ("row", "col"), split_axis=0, concat_axis=0, tiled=True)
    spread = spread.reshape(nrow, ncol, row_blocks, BS // nrow, col_blocks, BS // ncol)
    mirror = spread.transpose(2, 0, 3, 4, 1, 5).reshape(row_blocks, BS, col_blocks, BS)
    row_index = lax.axis_index("row")
    col_index = lax.axis_index("col")
    row_first = row_index * row_blocks
    col_first = col_index * col_blocks
    global_rows = row_first + jnp.arange(row_blocks, dtype=jnp.int32)
    global_cols = col_first + jnp.arange(col_blocks, dtype=jnp.int32)
    above = global_rows[:, None] < global_cols[None, :]
    below = global_rows[:, None] > global_cols[None, :]
    upper_pat = lax.dynamic_slice(pattern, (row_first, col_first), (row_blocks, col_blocks))
    lower_pat = lax.dynamic_slice(pattern, (col_first, row_first), (col_blocks, row_blocks)).T
    keep = jnp.where(above, upper_pat, jnp.where(below, lower_pat, 1)).astype(jnp.float32)
    own = upper.reshape(row_blocks, BS, col_blocks, BS)
    blended = jnp.where(
        above[:, None, :, None],
        own,
        jnp.where(below[:, None, :, None], mirror, 0.5 * (own + mirror)),
    )
    density = (blended * keep[:, None, :, None]).reshape(rows_tile, cols_tile)
    layer = lax.axis_index("depth")

    def layer_columns(tile):
        split = tile.reshape(rows_tile, col_blocks // ndep, ndep, BS)
        return lax.dynamic_slice_in_dim(split, layer, 1, 2).reshape(
            rows_tile, col_blocks // ndep * BS
        )

    split_rows = density.reshape(row_blocks // ndep, ndep, BS, cols_tile)
    layer_rows = lax.dynamic_slice_in_dim(split_rows, layer, 1, 1).reshape(
        row_blocks // ndep * BS, cols_tile
    )
    panel = lax.all_gather(layer_rows, "row", axis=0, tiled=True)

    def accumulate(piece):
        return jnp.dot(
            piece, panel, precision=lax.Precision.HIGHEST, preferred_element_type=jnp.float32
        )

    square_part = accumulate(lax.all_gather(layer_columns(density), "col", axis=1, tiled=True))
    square = lax.psum(square_part, "depth")
    cube_part = accumulate(lax.all_gather(layer_columns(square), "col", axis=1, tiled=True))
    cube = lax.psum(cube_part, "depth")
    return 3.0 * square - 2.0 * cube


def dense_halves(upper, pattern, *rest):
    whole = dense(upper, pattern)
    return whole, lax.dynamic_slice_in_dim(whole, lax.axis_index("depth") * MR, MR, 0)


def local(upper, pattern):
    stored, slot, first, last, fits = layout(pattern)
    blocks = gather(upper, pattern, first, last)
    lists = lax.optimization_barrier(work_lists(stored, slot))
    whole, mine = lax.cond(fits, multiply, dense_halves, upper, pattern, blocks, *lists)
    other = lax.ppermute(mine, "depth", [(0, 1), (1, 0)])
    return pl.pallas_call(
        join_kernel,
        out_shape=jax.ShapeDtypeStruct(upper.shape, jnp.float32),
        in_specs=[SMEM, ANY, ANY],
        out_specs=ANY,
        input_output_aliases={1: 0},
        scratch_shapes=[
            pltpu.VMEM((4, MR // 4, COLS * BS), jnp.float32),
            pltpu.SemaphoreType.DMA((4,)),
            pltpu.SemaphoreType.DMA((4,)),
        ],
        compiler_params=pltpu.CompilerParams(vmem_limit_bytes=16 * 1024 * 1024),
    )(lax.axis_index("depth")[None].astype(jnp.int32), whole, other)


def solution(mesh):
    placed = (P("row", "col"), P())
    return jax.shard_map(
        local, mesh=mesh, in_specs=placed, out_specs=P("row", "col"), check_vma=False
    )
```
